128 devices in a mesh: ctx: 32 (over y, z, core), ch: 4 (over x).
Axes of the slice: x: 4, y: 4, z: 4, core: 2. Of those that a mesh axis runs over, the one named last changes fastest.
Arguments:
- hyena_query: bfloat16 [4096, 4096], P('ctx', 'ch'), may hold values from -6 to 6
- hyena_key: bfloat16 [4096, 4096], P('ctx', 'ch'), may hold values from -6 to 6
- token_ids: int32 [4096], P('ctx'), may hold values from 0 to 511
- embed_table: bfloat16 [512, 4096], P(None, 'ch'), may hold values from -512 to 512
- norm_gain: float32 [4096], P('ch'), may hold values from 0.1 to 1.9
- hyena_filter: float32 [4096, 256], P('ctx', 'ch'), may hold values from -0.5 to 0.5
- attn_query: bfloat16 [4096, 4096], P('ctx', 'ch'), may hold values from -4.5 to 4.5
- attn_key: bfloat16 [4096, 4096], P('ctx', 'ch'), may hold values from -4.5 to 4.5
- document_ids: int32 [4096], P('ctx'), may hold values from 0 to 3, never falling along the last dimension, each value on 1 to 2048 neighbouring positions
Outputs:
- hyena_out: bfloat16 [4096, 4096], P('ctx', 'ch')
- attn_out: bfloat16 [4096, 4096], P('ctx', 'ch')
The draws below stay inside these ranges and needn't reach their ends.
Inputs may be any that keep to these rules, and one draw needn't show every extreme that they name: `document_ids`: never falls along the sequence.
All inputs are finite; a program needn't handle non-finite values.
Results may differ from the reference program's by a relative error of at most 0.018.
Values may be sent and summed in bfloat16 or wider, within the bound.
A program may use at most 128 MiB of HBM per device.

```python
import math
import jax
import jax.numpy as jnp
import numpy as np
from jax import lax

HEADS = 32
HEAD_DIM = 128
GROUP = 16
VOCAB = 512
GENOME_LETTERS = 4096
CHANNELS = 4096
FILTER_GROUPS = 256


def draw_attn_query(key, part):
    key = jax.random.fold_in(key, 31)
    values_field = jnp.clip(jax.random.normal(key, (GENOME_LETTERS, CHANNELS)), -4.5, 4.5)
    return values_field.astype(jnp.bfloat16)


def draw_attn_key(key, part):
    key = jax.random.fold_in(key, 37)
    values_field = jnp.clip(jax.random.normal(key, (GENOME_LETTERS, CHANNELS)), -4.5, 4.5)
    return values_field.astype(jnp.bfloat16)


def draw_embed_table(key, part):
    key = jax.random.fold_in(key, 23)
    subkeys = jax.random.split(key, 2)
    row_scale = jnp.exp(jax.random.uniform(subkeys[0], (VOCAB, 1), minval=0.0, maxval=math.log(10.0)))
    column_place = jnp.arange(CHANNELS, dtype=jnp.float32)[None, :] / CHANNELS
    column_scale = 10.0 ** column_place
    gaussian_jitter = jnp.clip(jax.random.normal(subkeys[1], (VOCAB, CHANNELS)), -4.0, 4.0)
    return (gaussian_jitter * row_scale * column_scale).astype(jnp.bfloat16)


def draw_hyena_filter(key, part):
    key = jax.random.fold_in(key, 11)
    subkeys = jax.random.split(key, 8)
    pulse_moments = jnp.arange(GENOME_LETTERS, dtype=jnp.float32)[:, None]
    decay_scale = jnp.exp(jax.random.uniform(subkeys[0], (1, FILTER_GROUPS), minval=math.log(30.0), maxval=math.log(4.0 * GENOME_LETTERS)))
    gaussian_jitter = jax.random.normal(subkeys[5], (GENOME_LETTERS, FILTER_GROUPS))
    tail_level = jax.random.uniform(subkeys[6], (1, FILTER_GROUPS), minval=0.04, maxval=0.08)
    tail_decay = jnp.exp(jax.random.uniform(subkeys[7], (1, FILTER_GROUPS), minval=math.log(4.0 * GENOME_LETTERS), maxval=math.log(16.0 * GENOME_LETTERS)))
    event_positions = jax.random.randint(subkeys[3], (3, FILTER_GROUPS), 0, GENOME_LETTERS)
    dropped_sites = jax.random.uniform(subkeys[4], (3, FILTER_GROUPS), minval=0.5, maxval=0.8)
    pulse_train = jnp.ones((GENOME_LETTERS, FILTER_GROUPS), jnp.float32)
    for spike_index in range(3):
        arrival_mask = pulse_moments >= event_positions[spike_index][None, :].astype(jnp.float32)
        pulse_train = pulse_train * jnp.where(arrival_mask, dropped_sites[spike_index][None, :], 1.0)
    pulse_height = jnp.sqrt(2.0 / jnp.minimum(decay_scale, float(GENOME_LETTERS)))
    envelope = jnp.exp(-pulse_moments / decay_scale) + tail_level * jnp.exp(-pulse_moments / tail_decay)
    return jnp.clip(pulse_height * envelope * pulse_train * gaussian_jitter, -0.5, 0.5)


def set_ends(values, stream_key, least, largest):
    extent = values.shape
    place = [jax.random.randint(jax.random.fold_in(stream_key, axis), (), 0, extent[axis]) for axis in range(len(extent))]
    values = values.at[tuple(place)].set(least)
    longest = extent.index(max(extent))
    place[longest] = (place[longest] + 1) % extent[longest]
    return values.at[tuple(place)].set(largest)


def block_scale(rng, extent, shards, smallest, top_value):
    level, own = 1.0, jax.random.fold_in(rng, 6)
    for axis_at, shards_of in shards:
        draws = jnp.exp(jax.random.uniform(jax.random.fold_in(own, axis_at), (shards_of,), jnp.float32, smallest / len(shards), top_value / len(shards)))
        level = level * jnp.repeat(draws, extent[axis_at] // shards_of).reshape([-1 if axis == axis_at else 1 for axis in range(len(extent))])
    return level


def split_up(count, total, bound, slope):
    loads = [(1 << 20) // math.isqrt(standing ** slope) + 1 for standing in range(2, count + 1)]
    spare, given = total - bound - (count - 1), [1] * (count - 1)
    while spare > 0:
        free = [i for i in range(count - 1) if given[i] < bound]
        pool, left = sum([loads[i] for i in free]), spare
        for i in free:
            more = min(bound - given[i], max(1, left * loads[i] // pool), spare)
            given[i] = given[i] + more
            spare = spare - more
    return np.array([bound] + given)


def uneven(key, amount, total, limit, skew):
    if amount == 2:
        one = jax.random.randint(key, (), max(1, total - limit), min(limit, total - 1) + 1)
        return jnp.stack([one, total - one])
    lengths = jnp.asarray(split_up(amount, total, limit, skew), jnp.int32)
    couples = (amount - 1) // 2
    donor, taker = lengths[1:1 + 2 * couples:2], lengths[2:2 + 2 * couples:2]
    room = jnp.minimum(donor - 1, limit - taker)
    moved = jax.random.randint(jax.random.fold_in(key, 1), (couples,), 0, 1 << 20) % (room + 1)
    lengths = lengths.at[1:1 + 2 * couples:2].set(donor - moved).at[2:2 + 2 * couples:2].set(taker + moved)
    return lengths[jax.random.permutation(jax.random.fold_in(key, 2), amount)]


def scatter_about(key, extent, spread, bound, shards=(), kind=jnp.bfloat16):
    values = spread * jax.random.normal(key, extent, jnp.float32)
    if shards:
        values = values * block_scale(key, extent, shards, -0.22, 0.18)
    return jnp.clip(values, -bound, bound).astype(kind)


def setup_inputs(seed: int = 0) -> dict:
    seeds = jax.random.split(jax.random.key(seed), 10)
    hyena_query = scatter_about(seeds[0], (GENOME_LETTERS, CHANNELS), 1.0, 6.0, ((0, 32), (1, 4)))
    hyena_key = scatter_about(seeds[1], (GENOME_LETTERS, CHANNELS), 1.0, 6.0, ((0, 32), (1, 4)))
    token_ids = set_ends(jax.random.randint(seeds[2], (GENOME_LETTERS,), 0, VOCAB), jax.random.fold_in(seeds[2], 1), 0, VOCAB - 1).astype(jnp.int32)
    embed_table = draw_embed_table(jax.random.fold_in(seeds[9], 71), 0)
    norm_gain = jnp.clip(1.0 + 0.18 * jax.random.normal(seeds[4], (CHANNELS,), jnp.float32), 0.1, 1.9)
    hyena_filter = draw_hyena_filter(jax.random.fold_in(seeds[9], 71), 0)
    attn_query = draw_attn_query(jax.random.fold_in(seeds[9], 71), 0)
    attn_key = draw_attn_key(jax.random.fold_in(seeds[9], 71), 0)
    document_ids = jnp.searchsorted(jnp.cumsum(uneven(seeds[8], 4, GENOME_LETTERS, GENOME_LETTERS // 2, 0)), jnp.arange(GENOME_LETTERS), side="right").astype(jnp.int32)
    return dict(hyena_query=hyena_query, hyena_key=hyena_key, token_ids=token_ids, embed_table=embed_table, norm_gain=norm_gain, hyena_filter=hyena_filter, attn_query=attn_query, attn_key=attn_key, document_ids=document_ids)


epsilon = 1e-06
masked_score = -1e+30

def hyena_mixer(hyena_query, hyena_key, token_ids, embed_table, norm_gain, hyena_filter):
    picked = embed_table[token_ids].astype(jnp.float32)
    mean_square = lax.optimization_barrier(jnp.mean(picked * picked, axis=1, keepdims=True))
    normed = picked * lax.rsqrt(mean_square + epsilon) * norm_gain
    source = hyena_key.astype(jnp.float32) * normed
    padded_length = 2 * GENOME_LETTERS
    source_spectrum = jnp.fft.rfft(source, n=padded_length, axis=0)
    filter_spectrum = jnp.repeat(jnp.fft.rfft(hyena_filter, n=padded_length, axis=0), GROUP, axis=1)
    convolved = jnp.fft.irfft(source_spectrum * filter_spectrum, n=padded_length, axis=0)[:GENOME_LETTERS]
    return (hyena_query.astype(jnp.float32) * convolved).astype(jnp.bfloat16)

def reference(hyena_query, hyena_key, token_ids, embed_table, norm_gain, hyena_filter, attn_query, attn_key, document_ids):
    hyena_out = hyena_mixer(hyena_query, hyena_key, token_ids, embed_table, norm_gain, hyena_filter)
    positions = jnp.arange(GENOME_LETTERS, dtype=jnp.int32)
    allowed = (positions[None, :] <= positions[:, None]) & (document_ids[None, :] == document_ids[:, None])
    score_scale = HEAD_DIM ** (-0.5)
    head_queries = attn_query.reshape(GENOME_LETTERS, HEADS, HEAD_DIM).transpose(1, 0, 2)
    head_keys = attn_key.reshape(GENOME_LETTERS, HEADS, HEAD_DIM).transpose(1, 0, 2)
    head_values = hyena_out.reshape(GENOME_LETTERS, HEADS, HEAD_DIM).transpose(1, 0, 2)

    def attend_head(operands):
        queries, keys_here, values_here = operands
        scores = jnp.dot(queries, keys_here.T, preferred_element_type=jnp.float32) * score_scale
        scores = jnp.where(allowed, scores, masked_score)
        top = lax.optimization_barrier(jnp.max(scores, axis=1, keepdims=True))
        weights = jnp.where(allowed, jnp.exp(scores - top), 0.0)
        total = lax.optimization_barrier(jnp.sum(weights, axis=1, keepdims=True))
        numerator = jnp.dot(weights.astype(jnp.bfloat16), values_here, preferred_element_type=jnp.float32)
        return (numerator / total).astype(jnp.bfloat16)
    attended = lax.map(attend_head, (head_queries, head_keys, head_values))
    attn_out = attended.transpose(1, 0, 2).reshape(GENOME_LETTERS, HEADS * HEAD_DIM)
    return (hyena_out, attn_out)
```

```python
import functools
import math

import jax
import jax.numpy as jnp
from jax import lax
from jax.experimental import pallas as pl
from jax.experimental.pallas import tpu as pltpu
from jax.sharding import PartitionSpec as P

MESH = pl.DeviceIdType.MESH
F32 = jnp.float32
BF16 = jnp.bfloat16

CTX = 32
CH = 4
ROWS = 128
WIDTH = 1024
VOCAB = 512
CHANNELS = 4096
OWN = 32
GROUP = 16
HEAD_DIM = 128
PAD = 2048
WINDOW = PAD + ROWS
EPSILON = 1e-06
MASKED = -1e30
EXPONENT = HEAD_DIM**-0.5 * math.log2(math.e)

META, SOURCE, GATE, QUERY, KEY, KEY_PAIR, VALUE_PAIR, HOME, ATTN, SQUARES = range(10)


def nt_dot(a, b):
    return lax.dot_general(a, b, (((1,), (1,)), ((), ())), preferred_element_type=F32)


def nn_dot(a, b):
    return jnp.dot(a, b, preferred_element_type=F32)


def halves(value):
    high = value.astype(BF16)
    return high, (value - high.astype(F32)).astype(BF16)


def kernel(
    ids_ref,
    docs_ref,
    table_ref,
    gain_ref,
    gate_ref,
    key_ref,
    filter_ref,
    attn_query_ref,
    attn_key_ref,
    hyena_out_ref,
    attn_out_ref,
    squares,
    meta_out,
    meta_in,
    source_out,
    source_in,
    gate_out,
    gate_in,
    toeplitz,
    sums,
    values_t,
    values,
    keys,
    queries,
    docs_row,
    home_in,
    attn_t,
    attn_in,
    send,
    recv,
    local,
):
    me = lax.axis_index("ctx")
    my_ch = lax.axis_index("ch")
    core = lax.rem(me, 2)
    mine = lax.div(me, 2)
    pair = me + 1 - 2 * core

    def remote(src, dst, kind, to):
        return pltpu.make_async_remote_copy(
            src_ref=src,
            dst_ref=dst,
            send_sem=send.at[kind],
            recv_sem=recv.at[kind],
            device_id=to,
            device_id_type=MESH,
        )

    def wait_in(ref, kind):
        pltpu.make_async_copy(ref, ref, recv.at[kind]).wait()

    def wait_out(ref, kind):
        pltpu.make_async_copy(ref, ref, send.at[kind]).wait()

    barrier = pltpu.get_barrier_semaphore()

    @pl.loop(1, CTX)
    def _(r):
        pl.semaphore_signal(
            barrier, inc=1, device_id={"ctx": lax.rem(me + r, CTX)}, device_id_type=MESH
        )

    for r in range(1, CH):
        pl.semaphore_signal(
            barrier, inc=1, device_id={"ch": lax.rem(my_ch + r, CH)}, device_id_type=MESH
        )

    by_lane = jnp.zeros((VOCAB, 128), F32)
    for tile in range(WIDTH // 128):
        part = table_ref[:, tile * 128 : (tile + 1) * 128].astype(F32)
        by_lane = by_lane + part * part
    high, low = halves(by_lane)
    ones = jnp.ones((8, 128), BF16)
    squares[my_ch] = nt_dot(ones, high) + nt_dot(ones, low)

    taps = jnp.concatenate([filter_ref[...], jnp.zeros((ROWS, 64), F32)], axis=1).T
    docs = docs_ref[...].astype(F32)
    for d in range(CTX):
        meta_out[d] = jnp.concatenate([taps[2 * d : 2 * d + 2], docs, docs], axis=0)
    meta_in[me] = meta_out[me]

    pl.semaphore_wait(barrier, CTX - 1 + CH - 1)

    for r in range(1, CH):
        to = lax.rem(my_ch + r, CH)
        remote(squares.at[my_ch], squares.at[my_ch], SQUARES, {"ch": to}).start()

    @pl.loop(1, CTX)
    def _(r):
        to = lax.rem(me + r, CTX)
        remote(meta_out.at[to], meta_in.at[me], META, {"ctx": to}).start()

    one_hot_t = (lax.broadcasted_iota(jnp.int32, (VOCAB, ROWS), 0) == ids_ref[...]).astype(F32)
    picked = nn_dot(one_hot_t.T.astype(BF16), table_ref[...])
    product_t = (picked * key_ref[...].astype(F32) * gain_ref[...]).T

    wait_in(squares.at[pl.ds(0, CH - 1)], SQUARES)
    total = squares[0] + squares[1] + squares[2] + squares[3]
    high, low = halves(total)
    one_hot_t = one_hot_t.astype(BF16)
    mean_square = (nn_dot(high, one_hot_t) + nn_dot(low, one_hot_t)) * (1.0 / CHANNELS)
    scale = lax.rsqrt(mean_square + EPSILON)[0:1]
    source_out[...] = (product_t * scale).astype(BF16).reshape(CTX, OWN, ROWS)
    source_in[me] = source_out[me]

    @pl.loop(1, CTX)
    def _(r):
        to = lax.rem(me + r, CTX)
        remote(source_out.at[to], source_in.at[me], SOURCE, {"ctx": to}).start()

    gate_out[...] = gate_ref[...].astype(F32).T.astype(BF16).reshape(CTX, OWN, ROWS)
    gate_in[me] = gate_out[me]

    @pl.loop(1, CTX)
    def _(r):
        to = lax.rem(me + r, CTX)
        remote(gate_out.at[to], gate_in.at[me], GATE, {"ctx": to}).start()

    my_keys = keys.at[pl.ds(PAD + me * ROWS, ROWS)]
    my_head = pl.ds(pl.multiple_of(lax.div(me, 4) * HEAD_DIM, HEAD_DIM), HEAD_DIM)
    own_key = pltpu.make_async_copy(attn_key_ref.at[:, my_head], my_keys, local.at[0])
    own_query = pltpu.make_async_copy(attn_query_ref.at[:, my_head], queries.at[mine], local.at[1])
    own_key.start()
    own_query.start()

    @pl.loop(1, CTX // 2)
    def _(r):
        to = lax.rem(me + 2 * r, CTX)
        head = pl.ds(pl.multiple_of(lax.div(to, 4) * HEAD_DIM, HEAD_DIM), HEAD_DIM)
        remote(attn_key_ref.at[:, head], my_keys, KEY, {"ctx": to}).start()

    @pl.loop(1, CTX // 2)
    def _(r):
        to = lax.rem(me + 2 * r, CTX)
        head = pl.ds(pl.multiple_of(lax.div(to, 4) * HEAD_DIM, HEAD_DIM), HEAD_DIM)
        remote(attn_query_ref.at[:, head], queries.at[mine], QUERY, {"ctx": to}).start()

    wait_in(meta_in.at[pl.ds(0, CTX - 1)], META)
    down = lax.broadcasted_iota(jnp.int32, (ROWS, ROWS), 0)
    right = lax.broadcasted_iota(jnp.int32, (ROWS, ROWS), 1)
    upper = right >= down

    def turned(n, g):
        row = jnp.broadcast_to(meta_in[n, g : g + 1, :], (ROWS, ROWS))
        return pltpu.roll(row, 0, 1, stride=1, stride_axis=0)

    for g in range(2):

        def build(k, carry):
            before, block_before = carry
            first = turned(2 * k, g)
            second = turned(2 * k + 1, g)
            block = jnp.where(upper, first, before).astype(BF16)
            block_next = jnp.where(upper, second, first).astype(BF16)
            toeplitz[g, k, 0:128, 0:128] = block
            toeplitz[g, k, 128:256, 128:256] = block
            toeplitz[g, k, 0:128, 128:256] = block_next
            toeplitz[g, k, 128:256, 0:128] = block_before
            return second, block_next

        lax.fori_loop(
            0, 16, build, (jnp.zeros((ROWS, ROWS), F32), jnp.zeros((ROWS, ROWS), BF16))
        )

    docs_row[:, 0:PAD] = jnp.full((8, PAD), -1.0, F32)
    for j in range(CTX):
        docs_row[:, PAD + j * ROWS : PAD + (j + 1) * ROWS] = jnp.broadcast_to(
            meta_in[j, 2:3, :], (8, ROWS)
        )
    values[0:PAD] = jnp.zeros((PAD, 128), BF16)
    keys[0:PAD] = jnp.zeros((PAD, 128), BF16)

    wait_in(source_in.at[pl.ds(0, CTX - 1)], SOURCE)
    for g in range(2):
        own = slice(g * GROUP, (g + 1) * GROUP)
        signal = source_in[:, own, :].reshape(16, 2, GROUP, ROWS)
        signal = jnp.concatenate(
            [signal[:, half].reshape(256, ROWS) for half in range(2)], axis=1
        )
        sums[g] = nn_dot(signal, toeplitz[g, 0])
        for k in range(1, 16):
            sums[g, 16 * k :] += nn_dot(signal[: 256 - 16 * k], toeplitz[g, k])

    wait_in(gate_in.at[pl.ds(0, CTX - 1)], GATE)
    for g in range(2):
        own = slice(g * GROUP, (g + 1) * GROUP)
        convolved = jnp.stack(
            [sums[g, :, half * ROWS : (half + 1) * ROWS].reshape(16, GROUP, ROWS) for half in range(2)],
            axis=1,
        ).reshape(CTX, GROUP, ROWS)
        values_t[core, :, own, :] = (convolved * gate_in[:, own, :].astype(F32)).astype(BF16)

    remote(values_t.at[core], values_t.at[core], VALUE_PAIR, {"ctx": pair}).start()

    own_key.wait()
    own_query.wait()
    wait_in(keys.at[pl.ds(0, 15 * ROWS)], KEY)

    @pl.loop(0, 16)
    def _(q):
        block = keys.at[pl.ds(PAD + (2 * q + core) * ROWS, ROWS)]
        remote(block, block, KEY_PAIR, {"ctx": pair}).start()

    @pl.loop(1, CTX)
    def _(r):
        to = lax.rem(me + r, CTX)
        block = values_t.at[core, to]
        remote(block, home_in.at[me], HOME, {"ctx": to}).start()

    home_in[me] = values_t[core, me]

    wait_in(queries.at[pl.ds(0, 15)], QUERY)
    wait_in(values_t.at[0], VALUE_PAIR)

    @pl.loop(0, CTX)
    def _(j):
        block = jnp.concatenate(
            [
                values_t[0, j].astype(F32),
                values_t[1, j].astype(F32),
                jnp.ones((64, ROWS), F32),
            ],
            axis=0,
        )
        values[pl.ds(pl.multiple_of(PAD + j * ROWS, ROWS), ROWS)] = block.T.astype(BF16)

    wait_in(keys.at[pl.ds(0, 16 * ROWS)], KEY_PAIR)

    @pl.loop(0, 16)
    def _(q):
        block = 2 * q + core
        start = pl.multiple_of(block * ROWS, ROWS)
        window = pl.ds(start, WINDOW)
        scores = nt_dot(queries[q], keys[window])
        own_docs = docs_row[0:1, pl.ds(pl.multiple_of(PAD + start, ROWS), ROWS)]
        own_docs = jnp.broadcast_to(own_docs, (ROWS, ROWS)).T[:, 0:1]
        allowed = docs_row[0:1, window] == own_docs
        causal = lax.broadcasted_iota(jnp.int32, (ROWS, WINDOW), 1) <= PAD + (
            lax.broadcasted_iota(jnp.int32, (ROWS, WINDOW), 0)
        )
        scores = jnp.where(allowed & causal, scores, MASKED)
        top = jnp.max(scores, axis=1, keepdims=True)
        weights = jnp.exp2((scores - top) * EXPONENT).astype(BF16)
        numerator = nn_dot(weights, values[window])
        result = numerator * (1.0 / numerator[:, 64:65])
        attn_t[q] = result.T[0:64].astype(BF16)

        @pl.when(block != me)
        def _():
            remote(attn_t.at[q], attn_in.at[mine], ATTN, {"ctx": block}).start()

        @pl.when(block == me)
        def _():
            attn_in[mine] = attn_t[q]

    wait_in(home_in.at[pl.ds(0, CTX - 1)], HOME)
    hyena_out_ref[...] = home_in[...].reshape(WIDTH, ROWS).astype(F32).T.astype(BF16)
    wait_in(attn_in.at[pl.ds(0, 15)], ATTN)
    attn_out_ref[...] = attn_in[...].reshape(WIDTH, ROWS).astype(F32).T.astype(BF16)

    wait_out(squares.at[pl.ds(0, CH - 1)], SQUARES)
    wait_out(meta_in.at[pl.ds(0, CTX - 1)], META)
    wait_out(source_out.at[pl.ds(0, CTX - 1)], SOURCE)
    wait_out(gate_out.at[pl.ds(0, CTX - 1)], GATE)
    wait_out(queries.at[pl.ds(0, 15)], QUERY)
    wait_out(keys.at[pl.ds(0, 15 * ROWS)], KEY)
    wait_out(keys.at[pl.ds(0, 16 * ROWS)], KEY_PAIR)
    wait_out(values_t.at[0], VALUE_PAIR)
    wait_out(home_in.at[pl.ds(0, CTX - 1)], HOME)
    wait_out(attn_in.at[pl.ds(0, 15)], ATTN)


def per_device(
    hyena_query,
    hyena_key,
    token_ids,
    embed_table,
    norm_gain,
    hyena_filter,
    attn_query,
    attn_key,
    document_ids,
):
    vmem = pl.BlockSpec(memory_space=pltpu.VMEM)
    hbm = pl.BlockSpec(memory_space=pl.ANY)
    shape = jax.ShapeDtypeStruct((ROWS, WIDTH), BF16)
    return pl.pallas_call(
        kernel,
        out_shape=(shape, shape),
        in_specs=[vmem] * 7 + [hbm] * 2,
        out_specs=(vmem, vmem),
        scratch_shapes=[
            pltpu.VMEM((CH, 8, VOCAB), F32),
            pltpu.VMEM((CTX, 4, ROWS), F32),
            pltpu.VMEM((CTX, 4, ROWS), F32),
            pltpu.VMEM((CTX, OWN, ROWS), BF16),
            pltpu.VMEM((CTX, OWN, ROWS), BF16),
            pltpu.VMEM((CTX, OWN, ROWS), BF16),
            pltpu.VMEM((CTX, OWN, ROWS), BF16),
            pltpu.VMEM((2, 16, 256, 256), BF16),
            pltpu.VMEM((2, 256, 256), F32),
            pltpu.VMEM((2, CTX, OWN, ROWS), BF16),
            pltpu.VMEM((PAD + CTX * ROWS, 128), BF16),
            pltpu.VMEM((PAD + CTX * ROWS, 128), BF16),
            pltpu.VMEM((16, ROWS, HEAD_DIM), BF16),
            pltpu.VMEM((8, PAD + CTX * ROWS), F32),
            pltpu.VMEM((CTX, OWN, ROWS), BF16),
            pltpu.VMEM((16, 64, ROWS), BF16),
            pltpu.VMEM((16, 64, ROWS), BF16),
            pltpu.SemaphoreType.DMA((10,)),
            pltpu.SemaphoreType.DMA((10,)),
            pltpu.SemaphoreType.DMA((2,)),
        ],
        compiler_params=pltpu.CompilerParams(
            collective_id=0, has_side_effects=True, vmem_limit_bytes=48 * 1024 * 1024
        ),
    )(
        token_ids.reshape(1, ROWS),
        document_ids.reshape(1, ROWS),
        embed_table,
        norm_gain.reshape(1, WIDTH),
        hyena_query,
        hyena_key,
        hyena_filter,
        attn_query,
        attn_key,
    )


def solution(mesh):
    placed = (
        P("ctx", "ch"),
        P("ctx", "ch"),
        P("ctx"),
        P(None, "ch"),
        P("ch"),
        P("ctx", "ch"),
        P("ctx", "ch"),
        P("ctx", "ch"),
        P("ctx"),
    )
    return jax.shard_map(
        per_device,
        mesh=mesh,
        in_specs=placed,
        out_specs=(P("ctx", "ch"), P("ctx", "ch")),
        check_vma=False,
    )
```

```python
import functools
import math

import jax
import jax.numpy as jnp
from jax import lax
from jax.experimental import pallas as pl
from jax.experimental.pallas import tpu as pltpu
from jax.sharding import PartitionSpec as P

MESH = pl.DeviceIdType.MESH
F32 = jnp.float32
BF16 = jnp.bfloat16

CTX = 32
CH = 4
ROWS = 128
WIDTH = 1024
VOCAB = 512
CHANNELS = 4096
OWN = 32
GROUP = 16
HEAD_DIM = 128
PAD = 2048
WINDOW = PAD + ROWS
EPSILON = 1e-06
MASKED = -1e30
EXPONENT = HEAD_DIM**-0.5 * math.log2(math.e)

META, SOURCE, GATE, QUERY, KEY, KEY_PAIR, VALUE_PAIR, HOME, ATTN, SQUARES = range(10)


def nt_dot(a, b):
    return lax.dot_general(a, b, (((1,), (1,)), ((), ())), preferred_element_type=F32)


def nn_dot(a, b):
    return jnp.dot(a, b, preferred_element_type=F32)


def halves(value):
    high = value.astype(BF16)
    return high, (value - high.astype(F32)).astype(BF16)


def kernel(
    ids_hbm,
    docs_hbm,
    table_hbm,
    gain_hbm,
    gate_hbm,
    key_hbm,
    filter_hbm,
    attn_query_ref,
    attn_key_ref,
    hyena_out_ref,
    attn_out_ref,
    ids_ref,
    docs_ref,
    table_ref,
    gain_ref,
    gate_ref,
    key_ref,
    filter_ref,
    squares,
    meta_out,
    meta_in,
    source_out,
    source_in,
    gate_out,
    gate_in,
    toeplitz,
    sums,
    values_t,
    keys,
    queries,
    docs_row,
    home_in,
    attn_t,
    attn_in,
    send,
    recv,
    local,
    key_recv,
    query_recv,
):
    me = lax.axis_index("ctx")
    my_ch = lax.axis_index("ch")
    core = lax.rem(me, 2)
    mine = lax.div(me, 2)
    pair = me + 1 - 2 * core

    def remote(src, dst, kind, to, arrived=None):
        return pltpu.make_async_remote_copy(
            src_ref=src,
            dst_ref=dst,
            send_sem=send.at[kind],
            recv_sem=recv.at[kind] if arrived is None else arrived,
            device_id=to,
            device_id_type=MESH,
        )

    def wait_in(ref, kind):
        pltpu.make_async_copy(ref, ref, recv.at[kind]).wait()

    def wait_out(ref, kind):
        pltpu.make_async_copy(ref, ref, send.at[kind]).wait()

    loads = [
        pltpu.make_async_copy(src, dst, local.at[at])
        for at, (src, dst) in enumerate(
            (
                (table_hbm, table_ref),
                (filter_hbm, filter_ref),
                (docs_hbm, docs_ref),
                (ids_hbm, ids_ref),
                (key_hbm, key_ref),
                (gain_hbm, gain_ref),
                (gate_hbm, gate_ref),
            )
        )
    ]
    for load in loads:
        load.start()

    my_keys = keys.at[pl.ds(PAD + me * ROWS, ROWS)]
    my_head = pl.ds(pl.multiple_of(lax.div(me, 4) * HEAD_DIM, HEAD_DIM), HEAD_DIM)
    pltpu.make_async_copy(attn_key_ref.at[:, my_head], my_keys, key_recv.at[0]).start()
    pltpu.make_async_copy(attn_query_ref.at[:, my_head], queries.at[mine], query_recv.at[0]).start()

    barrier = pltpu.get_barrier_semaphore()

    @pl.loop(1, CTX)
    def _(r):
        pl.semaphore_signal(
            barrier, inc=1, device_id={"ctx": lax.rem(me + r, CTX)}, device_id_type=MESH
        )

    for r in range(1, CH):
        pl.semaphore_signal(
            barrier, inc=1, device_id={"ch": lax.rem(my_ch + r, CH)}, device_id_type=MESH
        )

    for load in loads:
        load.wait()

    by_lane = jnp.zeros((VOCAB, 128), F32)
    for tile in range(WIDTH // 128):
        part = table_ref[:, tile * 128 : (tile + 1) * 128].astype(F32)
        by_lane = by_lane + part * part
    high, low = halves(by_lane)
    ones = jnp.ones((8, 128), BF16)
    squares[my_ch] = nt_dot(ones, high) + nt_dot(ones, low)

    taps = filter_ref[...]
    docs = docs_ref[...].astype(F32)
    for d in range(CTX):
        meta_out[d] = jnp.concatenate([taps[2 * d : 2 * d + 2], docs, docs], axis=0)
    meta_in[me] = meta_out[me]

    gate_out[...] = gate_ref[...].astype(F32).T.astype(BF16).reshape(CTX, OWN, ROWS)
    gate_in[me] = gate_out[me]
    docs_row[:, 0:PAD] = jnp.full((8, PAD), -1.0, F32)
    keys[0:PAD] = jnp.zeros((PAD, 128), BF16)
    values_t[0:64, 0:PAD] = jnp.zeros((64, PAD), BF16)
    values_t[64:80, :] = jnp.ones((16, PAD + CTX * ROWS), BF16)
    one_hot_t = (lax.broadcasted_iota(jnp.int32, (VOCAB, ROWS), 0) == ids_ref[...]).astype(F32)
    picked = nn_dot(one_hot_t.T.astype(BF16), table_ref[...])
    product_t = (picked * key_ref[...].astype(F32) * gain_ref[...]).T

    pl.semaphore_wait(barrier, CTX - 1 + CH - 1)

    for r in range(1, CH):
        to = lax.rem(my_ch + r, CH)
        remote(squares.at[my_ch], squares.at[my_ch], SQUARES, {"ch": to}).start()

    @pl.loop(1, CTX)
    def _(r):
        to = lax.rem(me + r, CTX)
        remote(meta_out.at[to], meta_in.at[me], META, {"ctx": to}).start()

    wait_in(squares.at[pl.ds(0, CH - 1)], SQUARES)
    total = squares[0] + squares[1] + squares[2] + squares[3]
    high, low = halves(total)
    one_hot_t = one_hot_t.astype(BF16)
    mean_square = (nn_dot(high, one_hot_t) + nn_dot(low, one_hot_t)) * (1.0 / CHANNELS)
    scale = lax.rsqrt(mean_square + EPSILON)[0:1]
    source_out[...] = (product_t * scale).astype(BF16).reshape(CTX, OWN, ROWS)
    source_in[me] = source_out[me]

    @pl.loop(1, CTX)
    def _(r):
        to = lax.rem(me + r, CTX)
        remote(source_out.at[to], source_in.at[me], SOURCE, {"ctx": to}).start()

    @pl.loop(1, CTX)
    def _(r):
        to = lax.rem(me + r, CTX)
        remote(gate_out.at[to], gate_in.at[me], GATE, {"ctx": to}).start()

    @pl.loop(1, CTX // 2)
    def _(r):
        to = lax.rem(me + 2 * r, CTX)
        head = pl.ds(pl.multiple_of(lax.div(to, 4) * HEAD_DIM, HEAD_DIM), HEAD_DIM)
        remote(attn_key_ref.at[:, head], my_keys, KEY, {"ctx": to}, key_recv.at[r]).start()

    @pl.loop(1, CTX // 2)
    def _(r):
        to = lax.rem(me + 2 * r, CTX)
        head = pl.ds(pl.multiple_of(lax.div(to, 4) * HEAD_DIM, HEAD_DIM), HEAD_DIM)
        remote(
            attn_query_ref.at[:, head], queries.at[mine], QUERY, {"ctx": to}, query_recv.at[r]
        ).start()

    wait_in(meta_in.at[pl.ds(0, CTX - 1)], META)
    down = lax.broadcasted_iota(jnp.int32, (ROWS, ROWS), 0)
    right = lax.broadcasted_iota(jnp.int32, (ROWS, ROWS), 1)
    upper = right >= down

    def turned(n, g):
        row = jnp.broadcast_to(meta_in[n, g : g + 1, :], (ROWS, ROWS))
        return pltpu.roll(row, 0, 1, stride=1, stride_axis=0)

    for g in range(2):

        def build(k, carry):
            before, block_before = carry
            first = turned(2 * k, g)
            second = turned(2 * k + 1, g)
            block = jnp.where(upper, first, before).astype(BF16)
            block_next = jnp.where(upper, second, first).astype(BF16)
            toeplitz[g, k, 0:128, 0:128] = block
            toeplitz[g, k, 128:256, 128:256] = block
            toeplitz[g, k, 0:128, 128:256] = block_next
            toeplitz[g, k, 128:256, 0:128] = block_before
            return second, block_next

        lax.fori_loop(
            0, 16, build, (jnp.zeros((ROWS, ROWS), F32), jnp.zeros((ROWS, ROWS), BF16))
        )

    for j in range(CTX):
        docs_row[:, PAD + j * ROWS : PAD + (j + 1) * ROWS] = jnp.broadcast_to(
            meta_in[j, 2:3, :], (8, ROWS)
        )

    wait_in(source_in.at[pl.ds(0, CTX - 1)], SOURCE)
    for g in range(2):
        own = slice(g * GROUP, (g + 1) * GROUP)
        signal = source_in[:, own, :].reshape(16, 2, GROUP, ROWS)
        signal = jnp.concatenate(
            [signal[:, half].reshape(256, ROWS) for half in range(2)], axis=1
        )
        sums[g] = nn_dot(signal, toeplitz[g, 0])
        for k in range(1, 16):
            sums[g, 16 * k :] += nn_dot(signal[: 256 - 16 * k], toeplitz[g, k])

    wait_in(gate_in.at[pl.ds(0, CTX - 1)], GATE)
    for g in range(2):
        own = slice(g * GROUP, (g + 1) * GROUP)
        rows = pl.ds(pl.multiple_of(OWN * core + GROUP * g, GROUP), GROUP)
        for j in range(16):
            gate = jnp.concatenate([gate_in[2 * j, own, :], gate_in[2 * j + 1, own, :]], axis=1)
            gated = sums[g, 16 * j : 16 * (j + 1)] * gate.astype(F32)
            values_t[rows, PAD + 256 * j : PAD + 256 * (j + 1)] = gated.astype(BF16)

    my_rows = pl.ds(pl.multiple_of(OWN * core, OWN), OWN)
    my_values = values_t.at[my_rows, pl.ds(PAD, CTX * ROWS)]
    remote(my_values, my_values, VALUE_PAIR, {"ctx": pair}).start()

    @pl.loop(0, CTX // 2)
    def _(r):
        source = lax.rem(me + CTX - 2 * r, CTX)
        block = keys.at[pl.ds(PAD + source * ROWS, ROWS)]
        pltpu.make_async_copy(block, block, key_recv.at[r]).wait()
        remote(block, block, KEY_PAIR, {"ctx": pair}).start()

    @pl.loop(1, CTX)
    def _(r):
        to = lax.rem(me + r, CTX)
        block = values_t.at[my_rows, pl.ds(pl.multiple_of(PAD + to * ROWS, ROWS), ROWS)]
        remote(block, home_in.at[me], HOME, {"ctx": to}).start()

    home_in[me] = values_t[my_rows, pl.ds(pl.multiple_of(PAD + me * ROWS, ROWS), ROWS)]

    wait_in(source_in, VALUE_PAIR)
    wait_in(keys.at[pl.ds(0, 16 * ROWS)], KEY_PAIR)

    def attend(q):
        start = pl.multiple_of((2 * q + core) * ROWS, ROWS)
        window = pl.ds(start, WINDOW)
        scores = nt_dot(queries[q], keys[window])
        own_docs = docs_row[0:1, pl.ds(pl.multiple_of(PAD + start, ROWS), ROWS)]
        own_docs = jnp.broadcast_to(own_docs, (ROWS, ROWS)).T[:, 0:1]
        same = docs_row[0:1, window] == own_docs
        past = jnp.where(same[:, :PAD], scores[:, :PAD], MASKED)
        diagonal = jnp.where(same[:, PAD:] & (down >= right), scores[:, PAD:], MASKED)
        scores = jnp.concatenate([past, diagonal], axis=1)
        top = jnp.max(scores, axis=1, keepdims=True)
        weights = jnp.exp2((scores - top) * EXPONENT).astype(BF16)
        numerator = nt_dot(values_t[:, window], weights)
        attn_t[q] = (numerator[0:64] * (1.0 / numerator[64:65])).astype(BF16)

    def give(q):
        block = 2 * q + core
        remote(attn_t.at[q], attn_in.at[mine], ATTN, {"ctx": block}).start()

    @pl.loop(0, 8)
    def _(p):
        places = [lax.rem(mine + 16 - 2 * p - at, 16) for at in range(2)]
        for at in range(2):
            block = queries.at[places[at]]
            pltpu.make_async_copy(block, block, query_recv.at[2 * p + at]).wait()
        for at in range(2):
            attend(places[at])

        @pl.when(p == 0)
        def _():
            attn_in[mine] = attn_t[mine]

        @pl.when(p > 0)
        def _():
            give(places[0])

        give(places[1])

    wait_in(home_in.at[pl.ds(0, CTX - 1)], HOME)
    hyena_out_ref[...] = home_in[...].reshape(WIDTH, ROWS).astype(F32).T.astype(BF16)
    wait_in(attn_in.at[pl.ds(0, 15)], ATTN)
    attn_out_ref[...] = attn_in[...].reshape(WIDTH, ROWS).astype(F32).T.astype(BF16)

    wait_out(squares.at[pl.ds(0, CH - 1)], SQUARES)
    wait_out(meta_in.at[pl.ds(0, CTX - 1)], META)
    wait_out(source_out.at[pl.ds(0, CTX - 1)], SOURCE)
    wait_out(gate_out.at[pl.ds(0, CTX - 1)], GATE)
    wait_out(queries.at[pl.ds(0, 15)], QUERY)
    wait_out(keys.at[pl.ds(0, 15 * ROWS)], KEY)
    wait_out(keys.at[pl.ds(0, 16 * ROWS)], KEY_PAIR)
    wait_out(source_in, VALUE_PAIR)
    wait_out(home_in.at[pl.ds(0, CTX - 1)], HOME)
    wait_out(attn_in.at[pl.ds(0, 15)], ATTN)


def per_device(
    hyena_query,
    hyena_key,
    token_ids,
    embed_table,
    norm_gain,
    hyena_filter,
    attn_query,
    attn_key,
    document_ids,
):
    vmem = pl.BlockSpec(memory_space=pltpu.VMEM)
    hbm = pl.BlockSpec(memory_space=pl.ANY)
    shape = jax.ShapeDtypeStruct((ROWS, WIDTH), BF16)
    return pl.pallas_call(
        kernel,
        out_shape=(shape, shape),
        in_specs=[hbm] * 9,
        out_specs=(vmem, vmem),
        scratch_shapes=[
            pltpu.VMEM((1, ROWS), jnp.int32),
            pltpu.VMEM((1, ROWS), jnp.int32),
            pltpu.VMEM((VOCAB, WIDTH), BF16),
            pltpu.VMEM((1, WIDTH), F32),
            pltpu.VMEM((ROWS, WIDTH), BF16),
            pltpu.VMEM((ROWS, WIDTH), BF16),
            pltpu.VMEM((64, ROWS), F32),
            pltpu.VMEM((CH, 8, VOCAB), F32),
            pltpu.VMEM((CTX, 4, ROWS), F32),
            pltpu.VMEM((CTX, 4, ROWS), F32),
            pltpu.VMEM((CTX, OWN, ROWS), BF16),
            pltpu.VMEM((CTX, OWN, ROWS), BF16),
            pltpu.VMEM((CTX, OWN, ROWS), BF16),
            pltpu.VMEM((CTX, OWN, ROWS), BF16),
            pltpu.VMEM((2, 16, 256, 256), BF16),
            pltpu.VMEM((2, 256, 256), F32),
            pltpu.VMEM((80, PAD + CTX * ROWS), BF16),
            pltpu.VMEM((PAD + CTX * ROWS, 128), BF16),
            pltpu.VMEM((16, ROWS, HEAD_DIM), BF16),
            pltpu.VMEM((8, PAD + CTX * ROWS), F32),
            pltpu.VMEM((CTX, OWN, ROWS), BF16),
            pltpu.VMEM((16, 64, ROWS), BF16),
            pltpu.VMEM((16, 64, ROWS), BF16),
            pltpu.SemaphoreType.DMA((10,)),
            pltpu.SemaphoreType.DMA((10,)),
            pltpu.SemaphoreType.DMA((7,)),
            pltpu.SemaphoreType.DMA((CTX // 2,)),
            pltpu.SemaphoreType.DMA((CTX // 2,)),
        ],
        compiler_params=pltpu.CompilerParams(
            collective_id=0, has_side_effects=True, vmem_limit_bytes=60 * 1024 * 1024
        ),
    )(
        token_ids.reshape(1, ROWS),
        document_ids.reshape(1, ROWS),
        embed_table,
        norm_gain.reshape(1, WIDTH),
        hyena_query,
        hyena_key,
        hyena_filter.T,
        attn_query,
        attn_key,
    )


def solution(mesh):
    placed = (
        P("ctx", "ch"),
        P("ctx", "ch"),
        P("ctx"),
        P(None, "ch"),
        P("ch"),
        P("ctx", "ch"),
        P("ctx", "ch"),
        P("ctx", "ch"),
        P("ctx"),
    )
    return jax.shard_map(
        per_device,
        mesh=mesh,
        in_specs=placed,
        out_specs=(P("ctx", "ch"), P("ctx", "ch")),
        check_vma=False,
    )
```

```python
import functools
import math

import jax
import jax.numpy as jnp
from jax import lax
from jax.experimental import pallas as pl
from jax.experimental.pallas import tpu as pltpu
from jax.sharding import PartitionSpec as P

MESH = pl.DeviceIdType.MESH
F32 = jnp.float32
BF16 = jnp.bfloat16

CTX = 32
CH = 4
ROWS = 128
WIDTH = 1024
VOCAB = 512
CHANNELS = 4096
OWN = 32
GROUP = 16
HEAD_DIM = 128
REACH = 2048
EPSILON = 1e-06
MASKED = -1e30
SAME = 8192.0
EXPONENT = HEAD_DIM**-0.5 * math.log2(math.e)

META, SOURCE, GATE, QUERY, KEY, KEY_PAIR, VALUE_PAIR, HOME, ATTN, SQUARES = range(10)


def nt_dot(a, b):
    return lax.dot_general(a, b, (((1,), (1,)), ((), ())), preferred_element_type=F32)


def nn_dot(a, b):
    return jnp.dot(a, b, preferred_element_type=F32)


def halves(value):
    high = value.astype(BF16)
    return high, (value - high.astype(F32)).astype(BF16)


def kernel(
    ids_hbm,
    docs_hbm,
    table_hbm,
    gain_hbm,
    gate_hbm,
    key_hbm,
    filter_hbm,
    attn_query_ref,
    attn_key_ref,
    hyena_out_ref,
    attn_out_ref,
    ids_ref,
    docs_ref,
    table_ref,
    gain_ref,
    gate_ref,
    key_ref,
    filter_ref,
    squares,
    ids_row,
    scales,
    signals,
    meta_out,
    meta_in,
    source_out,
    source_in,
    gate_out,
    gate_in,
    toeplitz,
    sums,
    values_t,
    keys,
    key_docs,
    queries,
    query_docs,
    home_in,
    attn_t,
    attn_in,
    send,
    recv,
    local,
    key_recv,
    query_recv,
):
    me = lax.axis_index("ctx")
    my_ch = lax.axis_index("ch")
    core = lax.rem(me, 2)
    mine = lax.div(me, 2)
    pair = me + 1 - 2 * core

    def remote(src, dst, kind, to, arrived=None):
        return pltpu.make_async_remote_copy(
            src_ref=src,
            dst_ref=dst,
            send_sem=send.at[kind],
            recv_sem=recv.at[kind] if arrived is None else arrived,
            device_id=to,
            device_id_type=MESH,
        )

    def wait_in(ref, kind):
        pltpu.make_async_copy(ref, ref, recv.at[kind]).wait()

    def wait_out(ref, kind):
        pltpu.make_async_copy(ref, ref, send.at[kind]).wait()

    loads = [
        pltpu.make_async_copy(src, dst, local.at[at])
        for at, (src, dst) in enumerate(
            (
                (table_hbm, table_ref),
                (filter_hbm, filter_ref),
                (docs_hbm, docs_ref),
                (ids_hbm, ids_ref),
                (key_hbm, key_ref),
                (gain_hbm, gain_ref),
                (gate_hbm, gate_ref),
            )
        )
    ]
    for load in loads:
        load.start()

    my_keys = keys.at[pl.ds(me * ROWS, ROWS)]
    my_queries = queries.at[mine]
    my_head = pl.ds(pl.multiple_of(lax.div(me, 4) * HEAD_DIM, HEAD_DIM), HEAD_DIM)
    pltpu.make_async_copy(attn_key_ref.at[:, my_head], my_keys, key_recv.at[0]).start()
    pltpu.make_async_copy(attn_query_ref.at[:, my_head], my_queries, query_recv.at[0]).start()

    barrier = pltpu.get_barrier_semaphore()

    @pl.loop(1, CTX)
    def _(r):
        pl.semaphore_signal(
            barrier, inc=1, device_id={"ctx": lax.rem(me + r, CTX)}, device_id_type=MESH
        )

    for r in range(1, CH):
        pl.semaphore_signal(
            barrier, inc=1, device_id={"ch": lax.rem(my_ch + r, CH)}, device_id_type=MESH
        )

    for load in loads[:6]:
        load.wait()

    taps = filter_ref[...]
    docs = docs_ref[...].astype(F32)
    ids = ids_ref[...].astype(F32)
    for d in range(CTX):
        meta_out[d] = jnp.concatenate([taps[2 * d : 2 * d + 2], docs, ids], axis=0)
    meta_in[me] = meta_out[me]

    one_hot_t = (lax.broadcasted_iota(jnp.int32, (VOCAB, ROWS), 0) == ids_ref[...]).astype(F32)
    picked = nn_dot(one_hot_t.T.astype(BF16), table_ref[...])
    product = picked * key_ref[...].astype(F32) * gain_ref[...]
    source_out[...] = product.T.astype(BF16).reshape(CTX, OWN, ROWS)
    source_in[me] = source_out[me]

    pl.semaphore_wait(barrier, CTX - 1 + CH - 1)

    @pl.loop(1, CTX)
    def _(r):
        to = lax.rem(me + r, CTX)
        remote(meta_out.at[to], meta_in.at[me], META, {"ctx": to}).start()

    @pl.loop(1, CTX)
    def _(r):
        to = lax.rem(me + r, CTX)
        remote(source_out.at[to], source_in.at[me], SOURCE, {"ctx": to}).start()

    by_lane = jnp.zeros((VOCAB, 128), F32)
    for tile in range(WIDTH // 128):
        part = table_ref[:, tile * 128 : (tile + 1) * 128].astype(F32)
        by_lane = by_lane + part * part
    high, low = halves(by_lane)
    ones = jnp.ones((8, 128), BF16)
    squares[my_ch] = nt_dot(ones, high) + nt_dot(ones, low)

    for r in range(1, CH):
        to = lax.rem(my_ch + r, CH)
        remote(squares.at[my_ch], squares.at[my_ch], SQUARES, {"ch": to}).start()

    loads[6].wait()
    gate_out[...] = gate_ref[...].astype(F32).T.astype(BF16).reshape(CTX, OWN, ROWS)
    gate_in[me] = gate_out[me]

    @pl.loop(1, CTX)
    def _(r):
        to = lax.rem(me + r, CTX)
        remote(gate_out.at[to], gate_in.at[me], GATE, {"ctx": to}).start()

    @pl.loop(1, CTX // 2)
    def _(r):
        to = lax.rem(me + 2 * r, CTX)
        head = pl.ds(pl.multiple_of(lax.div(to, 4) * HEAD_DIM, HEAD_DIM), HEAD_DIM)
        remote(attn_key_ref.at[:, head], my_keys, KEY, {"ctx": to}, key_recv.at[r]).start()

    @pl.loop(1, CTX // 2)
    def _(r):
        to = lax.rem(me + 2 * r, CTX)
        head = pl.ds(pl.multiple_of(lax.div(to, 4) * HEAD_DIM, HEAD_DIM), HEAD_DIM)
        remote(
            attn_query_ref.at[:, head], my_queries, QUERY, {"ctx": to}, query_recv.at[r]
        ).start()

    values_t[64:80, :] = jnp.ones((16, CTX * ROWS), BF16)

    wait_in(meta_in.at[pl.ds(0, CTX - 1)], META)
    down = lax.broadcasted_iota(jnp.int32, (ROWS, ROWS), 0)
    right = lax.broadcasted_iota(jnp.int32, (ROWS, ROWS), 1)
    upper = right >= down

    def turned(n, g):
        row = jnp.broadcast_to(meta_in[n, g : g + 1, :], (ROWS, ROWS))
        return pltpu.roll(row, 0, 1, stride=1, stride_axis=0)

    for g in range(2):

        def build(k, carry):
            before, block_before = carry
            first = turned(2 * k, g)
            second = turned(2 * k + 1, g)
            block = jnp.where(upper, first, before).astype(BF16)
            block_next = jnp.where(upper, second, first).astype(BF16)
            toeplitz[g, k, 0:128, 0:128] = block
            toeplitz[g, k, 128:256, 128:256] = block
            toeplitz[g, k, 0:128, 128:256] = block_next
            toeplitz[g, k, 128:256, 0:128] = block_before
            return second, block_next

        lax.fori_loop(
            0, 16, build, (jnp.zeros((ROWS, ROWS), F32), jnp.zeros((ROWS, ROWS), BF16))
        )

    @pl.loop(0, CTX)
    def _(j):
        which = down.astype(F32) == meta_in[j, 2:3, :]
        key_docs[pl.ds(pl.multiple_of(j * ROWS, ROWS), ROWS)] = (
            which.astype(F32).T.astype(BF16)
        )

    @pl.loop(0, 16)
    def _(q):
        rows = pl.ds(pl.multiple_of((2 * q + core) * ROWS, ROWS), ROWS)
        query_docs[q] = (key_docs[rows].astype(F32) * SAME).astype(BF16)

    for j in range(CTX):
        ids_row[:, j * ROWS : (j + 1) * ROWS] = meta_in[j, 3:4, :].astype(jnp.int32)
    wait_in(squares.at[pl.ds(0, CH - 1)], SQUARES)
    total = (squares[0] + squares[1] + squares[2] + squares[3])[0:1]
    low_digit = lax.broadcasted_iota(jnp.int32, (16, VOCAB), 0)
    token = lax.broadcasted_iota(jnp.int32, (16, VOCAB), 1)
    high, low = halves(jnp.where(lax.rem(token, 16) == low_digit, total, 0.0))
    high_digit = lax.broadcasted_iota(jnp.int32, (32, VOCAB), 0)
    token = lax.broadcasted_iota(jnp.int32, (32, VOCAB), 1)
    gather = (lax.div(token, 16) == high_digit).astype(F32).astype(BF16)
    high, low = halves(nt_dot(high, gather) + nt_dot(low, gather))
    digits = lax.div(ids_row[...], 16)
    chosen = lax.broadcasted_iota(jnp.int32, (32, CTX * ROWS), 0) == digits
    chosen = chosen.astype(F32).astype(BF16)
    choices = nn_dot(high, chosen) + nn_dot(low, chosen)
    digits = lax.rem(ids_row[...], 16)
    chosen = lax.broadcasted_iota(jnp.int32, (16, CTX * ROWS), 0) == digits
    square = jnp.sum(jnp.where(chosen, choices, 0.0), axis=0, keepdims=True)
    scales[...] = lax.rsqrt(square * (1.0 / CHANNELS) + EPSILON)

    wait_in(source_in.at[pl.ds(0, CTX - 1)], SOURCE)
    for j in range(CTX):
        scaled = source_in[j].astype(F32) * scales[:, j * ROWS : (j + 1) * ROWS]
        scaled = scaled.astype(BF16)
        lanes = slice(j % 2 * ROWS, (j % 2 + 1) * ROWS)
        for g in range(2):
            signals[g, j // 2 * GROUP : (j // 2 + 1) * GROUP, lanes] = scaled[
                g * GROUP : (g + 1) * GROUP
            ]
    for g in range(2):
        signal = signals[g]
        sums[g] = nn_dot(signal, toeplitz[g, 0])
        for k in range(1, 16):
            sums[g, 16 * k :] += nn_dot(signal[: 256 - 16 * k], toeplitz[g, k])

    wait_in(gate_in.at[pl.ds(0, CTX - 1)], GATE)
    for g in range(2):
        own = slice(g * GROUP, (g + 1) * GROUP)
        rows = pl.ds(pl.multiple_of(OWN * core + GROUP * g, GROUP), GROUP)
        for j in range(16):
            gate = jnp.concatenate([gate_in[2 * j, own, :], gate_in[2 * j + 1, own, :]], axis=1)
            gated = sums[g, 16 * j : 16 * (j + 1)] * gate.astype(F32)
            values_t[rows, 256 * j : 256 * (j + 1)] = gated.astype(BF16)

    my_rows = pl.ds(pl.multiple_of(OWN * core, OWN), OWN)
    my_values = values_t.at[my_rows, pl.ds(0, CTX * ROWS)]
    remote(my_values, my_values, VALUE_PAIR, {"ctx": pair}).start()

    @pl.loop(0, CTX // 2)
    def _(r):
        source = lax.rem(me + CTX - 2 * r, CTX)
        block = keys.at[pl.ds(source * ROWS, ROWS)]
        pltpu.make_async_copy(block, block, key_recv.at[r]).wait()
        remote(block, block, KEY_PAIR, {"ctx": pair}).start()

    @pl.loop(1, CTX)
    def _(r):
        to = lax.rem(me + r, CTX)
        block = values_t.at[my_rows, pl.ds(pl.multiple_of(to * ROWS, ROWS), ROWS)]
        remote(block, home_in.at[me], HOME, {"ctx": to}).start()

    home_in[me] = values_t[my_rows, pl.ds(pl.multiple_of(me * ROWS, ROWS), ROWS)]

    wait_in(source_in, VALUE_PAIR)
    wait_in(keys.at[pl.ds(0, 16 * ROWS)], KEY_PAIR)

    def attend(u, start, blocks, clear):
        rows = pl.ds(pl.multiple_of(start, ROWS), blocks * ROWS)
        some_keys = jnp.concatenate([keys[rows], key_docs[rows]], axis=1)
        both = pl.ds(2 * u, 2)
        some_queries = jnp.concatenate([queries[both], query_docs[both]], axis=2)
        scores = nt_dot(some_keys, some_queries.reshape(2 * ROWS, 256))
        shape = ((blocks - clear) * ROWS, 2 * ROWS)
        at_key = lax.broadcasted_iota(jnp.int32, shape, 0) + (start + clear * ROWS)
        at_query = lax.broadcasted_iota(jnp.int32, shape, 1)
        at_query = jnp.where(at_query >= ROWS, at_query + ROWS, at_query) + (4 * u + core) * ROWS
        late = jnp.where(at_key <= at_query, scores[clear * ROWS :], MASKED)
        if clear:
            late = jnp.concatenate([scores[: clear * ROWS], late], axis=0)
        top = jnp.max(late, axis=0, keepdims=True)
        weights = jnp.exp2((late - top) * EXPONENT).astype(BF16)
        numerator = nn_dot(values_t[:, rows], weights)
        result = (numerator[0:64] * (1.0 / numerator[64:65])).astype(BF16)
        attn_t[2 * u] = result[:, :ROWS]
        attn_t[2 * u + 1] = result[:, ROWS:]

    def give(q):
        block = 2 * q + core

        @pl.when(q == mine)
        def _():
            attn_in[mine] = attn_t[q]

        @pl.when(q != mine)
        def _():
            remote(attn_t.at[q], attn_in.at[mine], ATTN, {"ctx": block}).start()

    @pl.loop(0, 8)
    def _(p):
        u = lax.rem(lax.div(mine + 1, 2) + 7 - p, 8)
        for at in range(2):
            block = queries.at[2 * u + at]
            arrived = query_recv.at[lax.rem(mine + 16 - 2 * u - at, 16)]
            pltpu.make_async_copy(block, block, arrived).wait()

        @pl.when(u < 2)
        def _():
            attend(u, 0, 8, 0)

        @pl.when((u >= 2) & (u < 4))
        def _():
            attend(u, 0, 16, 8)

        @pl.when(u >= 4)
        def _():
            attend(u, (4 * u + core) * ROWS - REACH, 19, 16)

        give(2 * u)
        give(2 * u + 1)

    wait_in(home_in.at[pl.ds(0, CTX - 1)], HOME)
    hyena_out_ref[...] = home_in[...].reshape(WIDTH, ROWS).astype(F32).T.astype(BF16)
    wait_in(attn_in.at[pl.ds(0, 15)], ATTN)
    attn_out_ref[...] = attn_in[...].reshape(WIDTH, ROWS).astype(F32).T.astype(BF16)

    wait_out(squares.at[pl.ds(0, CH - 1)], SQUARES)
    wait_out(meta_in.at[pl.ds(0, CTX - 1)], META)
    wait_out(source_out.at[pl.ds(0, CTX - 1)], SOURCE)
    wait_out(gate_out.at[pl.ds(0, CTX - 1)], GATE)
    wait_out(queries.at[pl.ds(0, 15)], QUERY)
    wait_out(keys.at[pl.ds(0, 15 * ROWS)], KEY)
    wait_out(keys.at[pl.ds(0, 16 * ROWS)], KEY_PAIR)
    wait_out(source_in, VALUE_PAIR)
    wait_out(home_in.at[pl.ds(0, CTX - 1)], HOME)
    wait_out(attn_in.at[pl.ds(0, 15)], ATTN)


def per_device(
    hyena_query,
    hyena_key,
    token_ids,
    embed_table,
    norm_gain,
    hyena_filter,
    attn_query,
    attn_key,
    document_ids,
):
    vmem = pl.BlockSpec(memory_space=pltpu.VMEM)
    hbm = pl.BlockSpec(memory_space=pl.ANY)
    shape = jax.ShapeDtypeStruct((ROWS, WIDTH), BF16)
    return pl.pallas_call(
        kernel,
        out_shape=(shape, shape),
        in_specs=[hbm] * 9,
        out_specs=(vmem, vmem),
        scratch_shapes=[
            pltpu.VMEM((1, ROWS), jnp.int32),
            pltpu.VMEM((1, ROWS), jnp.int32),
            pltpu.VMEM((VOCAB, WIDTH), BF16),
            pltpu.VMEM((1, WIDTH), F32),
            pltpu.VMEM((ROWS, WIDTH), BF16),
            pltpu.VMEM((ROWS, WIDTH), BF16),
            pltpu.VMEM((64, ROWS), F32),
            pltpu.VMEM((CH, 8, VOCAB), F32),
            pltpu.VMEM((1, CTX * ROWS), jnp.int32),
            pltpu.VMEM((1, CTX * ROWS), F32),
            pltpu.VMEM((2, 256, 256), BF16),
            pltpu.VMEM((CTX, 4, ROWS), F32),
            pltpu.VMEM((CTX, 4, ROWS), F32),
            pltpu.VMEM((CTX, OWN, ROWS), BF16),
            pltpu.VMEM((CTX, OWN, ROWS), BF16),
            pltpu.VMEM((CTX, OWN, ROWS), BF16),
            pltpu.VMEM((CTX, OWN, ROWS), BF16),
            pltpu.VMEM((2, 16, 256, 256), BF16),
            pltpu.VMEM((2, 256, 256), F32),
            pltpu.VMEM((80, CTX * ROWS), BF16),
            pltpu.VMEM((CTX * ROWS, 128), BF16),
            pltpu.VMEM((CTX * ROWS, 128), BF16),
            pltpu.VMEM((16, ROWS, HEAD_DIM), BF16),
            pltpu.VMEM((16, ROWS, HEAD_DIM), BF16),
            pltpu.VMEM((CTX, OWN, ROWS), BF16),
            pltpu.VMEM((16, 64, ROWS), BF16),
            pltpu.VMEM((16, 64, ROWS), BF16),
            pltpu.SemaphoreType.DMA((10,)),
            pltpu.SemaphoreType.DMA((10,)),
            pltpu.SemaphoreType.DMA((7,)),
            pltpu.SemaphoreType.DMA((CTX // 2,)),
            pltpu.SemaphoreType.DMA((CTX // 2,)),
        ],
        compiler_params=pltpu.CompilerParams(
            collective_id=0, has_side_effects=True, vmem_limit_bytes=60 * 1024 * 1024
        ),
    )(
        token_ids.reshape(1, ROWS),
        document_ids.reshape(1, ROWS),
        embed_table,
        norm_gain.reshape(1, WIDTH),
        hyena_query,
        hyena_key,
        hyena_filter.T,
        attn_query,
        attn_key,
    )


def solution(mesh):
    placed = (
        P("ctx", "ch"),
        P("ctx", "ch"),
        P("ctx"),
        P(None, "ch"),
        P("ch"),
        P("ctx", "ch"),
        P("ctx", "ch"),
        P("ctx", "ch"),
        P("ctx"),
    )
    return jax.shard_map(
        per_device,
        mesh=mesh,
        in_specs=placed,
        out_specs=(P("ctx", "ch"), P("ctx", "ch")),
        check_vma=False,
    )
```

```python
import functools
import math

import jax
import jax.numpy as jnp
from jax import lax
from jax.experimental import pallas as pl
from jax.experimental.pallas import tpu as pltpu
from jax.sharding import PartitionSpec as P

MESH = pl.DeviceIdType.MESH
F32 = jnp.float32
BF16 = jnp.bfloat16

CTX = 32
CH = 4
ROWS = 128
WIDTH = 1024
VOCAB = 512
CHANNELS = 4096
OWN = 32
GROUP = 16
HEAD_DIM = 128
REACH = 2048
EPSILON = 1e-06
MASKED = -1e30
SAME = 8192.0
EXPONENT = HEAD_DIM**-0.5 * math.log2(math.e)

META, SOURCE, GATE, QUERY, KEY, KEY_PAIR, VALUE_PAIR, HOME, ATTN, SQUARES = range(10)


def nt_dot(a, b):
    return lax.dot_general(a, b, (((1,), (1,)), ((), ())), preferred_element_type=F32)


def nn_dot(a, b):
    return jnp.dot(a, b, preferred_element_type=F32)


def halves(value):
    high = value.astype(BF16)
    return high, (value - high.astype(F32)).astype(BF16)


def kernel(
    ids_hbm,
    docs_hbm,
    table_hbm,
    gain_hbm,
    gate_hbm,
    key_hbm,
    filter_hbm,
    attn_query_ref,
    attn_key_ref,
    home_in,
    attn_in,
    ids_ref,
    docs_ref,
    table_ref,
    gain_ref,
    gate_ref,
    key_ref,
    filter_ref,
    squares,
    ids_row,
    scales,
    signals,
    meta_out,
    meta_in,
    source_out,
    source_in,
    gate_out,
    gate_in,
    toeplitz,
    sums,
    values_t,
    keys,
    key_docs,
    queries,
    query_docs,
    attn_t,
    send,
    recv,
    local,
    key_recv,
    query_recv,
):
    me = lax.axis_index("ctx")
    my_ch = lax.axis_index("ch")
    core = lax.rem(me, 2)
    mine = lax.div(me, 2)
    pair = me + 1 - 2 * core

    def remote(src, dst, kind, to, arrived=None):
        return pltpu.make_async_remote_copy(
            src_ref=src,
            dst_ref=dst,
            send_sem=send.at[kind],
            recv_sem=recv.at[kind] if arrived is None else arrived,
            device_id=to,
            device_id_type=MESH,
        )

    def wait_in(ref, kind):
        pltpu.make_async_copy(ref, ref, recv.at[kind]).wait()

    def wait_out(ref, kind):
        pltpu.make_async_copy(ref, ref, send.at[kind]).wait()

    loads = [
        pltpu.make_async_copy(src, dst, local.at[at])
        for at, (src, dst) in enumerate(
            (
                (table_hbm, table_ref),
                (filter_hbm, filter_ref),
                (docs_hbm, docs_ref),
                (ids_hbm, ids_ref),
                (key_hbm, key_ref),
                (gain_hbm, gain_ref),
                (gate_hbm, gate_ref),
            )
        )
    ]
    for load in loads:
        load.start()

    my_keys = keys.at[pl.ds(me * ROWS, ROWS)]
    my_queries = queries.at[mine]
    my_head = pl.ds(pl.multiple_of(lax.div(me, 4) * HEAD_DIM, HEAD_DIM), HEAD_DIM)
    pltpu.make_async_copy(attn_key_ref.at[:, my_head], my_keys, key_recv.at[0]).start()
    pltpu.make_async_copy(attn_query_ref.at[:, my_head], my_queries, query_recv.at[0]).start()

    barrier = pltpu.get_barrier_semaphore()

    @pl.loop(1, CTX)
    def _(r):
        pl.semaphore_signal(
            barrier, inc=1, device_id={"ctx": lax.rem(me + r, CTX)}, device_id_type=MESH
        )

    for r in range(1, CH):
        pl.semaphore_signal(
            barrier, inc=1, device_id={"ch": lax.rem(my_ch + r, CH)}, device_id_type=MESH
        )

    for load in loads[:6]:
        load.wait()

    taps = filter_ref[...]
    docs = docs_ref[...].astype(F32)
    ids = ids_ref[...].astype(F32)
    for d in range(CTX):
        meta_out[d] = jnp.concatenate([taps[2 * d : 2 * d + 2], docs, ids], axis=0)
    meta_in[me] = meta_out[me]

    one_hot_t = (lax.broadcasted_iota(jnp.int32, (VOCAB, ROWS), 0) == ids_ref[...]).astype(F32)
    picked = nn_dot(one_hot_t.T.astype(BF16), table_ref[...])
    product = picked * key_ref[...].astype(F32) * gain_ref[...]
    source_out[...] = product.T.astype(BF16).reshape(CTX, OWN, ROWS)
    source_in[me] = source_out[me]

    pl.semaphore_wait(barrier, CTX - 1 + CH - 1)

    @pl.loop(1, CTX)
    def _(r):
        to = lax.rem(me + r, CTX)
        remote(meta_out.at[to], meta_in.at[me], META, {"ctx": to}).start()

    @pl.loop(1, CTX)
    def _(r):
        to = lax.rem(me + r, CTX)
        remote(source_out.at[to], source_in.at[me], SOURCE, {"ctx": to}).start()

    by_lane = jnp.zeros((VOCAB, 128), F32)
    for tile in range(WIDTH // 128):
        part = table_ref[:, tile * 128 : (tile + 1) * 128].astype(F32)
        by_lane = by_lane + part * part
    high, low = halves(by_lane)
    ones = jnp.ones((8, 128), BF16)
    squares[my_ch] = nt_dot(ones, high) + nt_dot(ones, low)

    for r in range(1, CH):
        to = lax.rem(my_ch + r, CH)
        remote(squares.at[my_ch], squares.at[my_ch], SQUARES, {"ch": to}).start()

    loads[6].wait()
    gate_out[...] = gate_ref[...].astype(F32).T.astype(BF16).reshape(CTX, OWN, ROWS)
    gate_in[me] = gate_out[me]

    @pl.loop(1, CTX)
    def _(r):
        to = lax.rem(me + r, CTX)
        remote(gate_out.at[to], gate_in.at[me], GATE, {"ctx": to}).start()

    @pl.loop(1, CTX // 2)
    def _(r):
        to = lax.rem(me + 2 * r, CTX)
        head = pl.ds(pl.multiple_of(lax.div(to, 4) * HEAD_DIM, HEAD_DIM), HEAD_DIM)
        remote(attn_key_ref.at[:, head], my_keys, KEY, {"ctx": to}, key_recv.at[r]).start()

    @pl.loop(1, CTX // 2)
    def _(r):
        to = lax.rem(me + 2 * r, CTX)
        head = pl.ds(pl.multiple_of(lax.div(to, 4) * HEAD_DIM, HEAD_DIM), HEAD_DIM)
        remote(
            attn_query_ref.at[:, head], my_queries, QUERY, {"ctx": to}, query_recv.at[r]
        ).start()

    values_t[64:80, :] = jnp.ones((16, CTX * ROWS), BF16)

    wait_in(meta_in.at[pl.ds(0, CTX - 1)], META)
    down = lax.broadcasted_iota(jnp.int32, (ROWS, ROWS), 0)
    right = lax.broadcasted_iota(jnp.int32, (ROWS, ROWS), 1)
    upper = right >= down

    def turned(n, g):
        row = jnp.broadcast_to(meta_in[n, g : g + 1, :], (ROWS, ROWS))
        return pltpu.roll(row, 0, 1, stride=1, stride_axis=0)

    for g in range(2):

        def build(k, carry):
            before, block_before = carry
            first = turned(2 * k, g)
            second = turned(2 * k + 1, g)
            block = jnp.where(upper, first, before).astype(BF16)
            block_next = jnp.where(upper, second, first).astype(BF16)
            toeplitz[g, k, 0:128, 0:128] = block
            toeplitz[g, k, 128:256, 128:256] = block
            toeplitz[g, k, 0:128, 128:256] = block_next
            toeplitz[g, k, 128:256, 0:128] = block_before
            return second, block_next

        lax.fori_loop(
            0, 16, build, (jnp.zeros((ROWS, ROWS), F32), jnp.zeros((ROWS, ROWS), BF16))
        )

    @pl.loop(0, CTX)
    def _(j):
        which = down.astype(F32) == meta_in[j, 2:3, :]
        key_docs[pl.ds(pl.multiple_of(j * ROWS, ROWS), ROWS)] = (
            which.astype(F32).T.astype(BF16)
        )

    @pl.loop(0, 16)
    def _(q):
        rows = pl.ds(pl.multiple_of((2 * q + core) * ROWS, ROWS), ROWS)
        query_docs[q] = (key_docs[rows].astype(F32) * SAME).astype(BF16)

    for j in range(CTX):
        ids_row[:, j * ROWS : (j + 1) * ROWS] = meta_in[j, 3:4, :].astype(jnp.int32)
    wait_in(squares.at[pl.ds(0, CH - 1)], SQUARES)
    total = (squares[0] + squares[1] + squares[2] + squares[3])[0:1]
    low_digit = lax.broadcasted_iota(jnp.int32, (16, VOCAB), 0)
    token = lax.broadcasted_iota(jnp.int32, (16, VOCAB), 1)
    high, low = halves(jnp.where(lax.rem(token, 16) == low_digit, total, 0.0))
    high_digit = lax.broadcasted_iota(jnp.int32, (32, VOCAB), 0)
    token = lax.broadcasted_iota(jnp.int32, (32, VOCAB), 1)
    gather = (lax.div(token, 16) == high_digit).astype(F32).astype(BF16)
    high, low = halves(nt_dot(high, gather) + nt_dot(low, gather))
    digits = lax.div(ids_row[...], 16)
    chosen = lax.broadcasted_iota(jnp.int32, (32, CTX * ROWS), 0) == digits
    chosen = chosen.astype(F32).astype(BF16)
    choices = nn_dot(high, chosen) + nn_dot(low, chosen)
    digits = lax.rem(ids_row[...], 16)
    chosen = lax.broadcasted_iota(jnp.int32, (16, CTX * ROWS), 0) == digits
    square = jnp.sum(jnp.where(chosen, choices, 0.0), axis=0, keepdims=True)
    scales[...] = lax.rsqrt(square * (1.0 / CHANNELS) + EPSILON)

    wait_in(source_in.at[pl.ds(0, CTX - 1)], SOURCE)
    for j in range(CTX):
        scaled = source_in[j].astype(F32) * scales[:, j * ROWS : (j + 1) * ROWS]
        scaled = scaled.astype(BF16)
        lanes = slice(j % 2 * ROWS, (j % 2 + 1) * ROWS)
        for g in range(2):
            signals[g, j // 2 * GROUP : (j // 2 + 1) * GROUP, lanes] = scaled[
                g * GROUP : (g + 1) * GROUP
            ]
    for g in range(2):
        signal = signals[g]
        sums[g] = nn_dot(signal, toeplitz[g, 0])
        for k in range(1, 16):
            sums[g, 16 * k :] += nn_dot(signal[: 256 - 16 * k], toeplitz[g, k])

    wait_in(gate_in.at[pl.ds(0, CTX - 1)], GATE)
    for g in range(2):
        own = slice(g * GROUP, (g + 1) * GROUP)
        rows = pl.ds(pl.multiple_of(OWN * core + GROUP * g, GROUP), GROUP)
        for j in range(16):
            gate = jnp.concatenate([gate_in[2 * j, own, :], gate_in[2 * j + 1, own, :]], axis=1)
            gated = sums[g, 16 * j : 16 * (j + 1)] * gate.astype(F32)
            values_t[rows, 256 * j : 256 * (j + 1)] = gated.astype(BF16)

    my_rows = pl.ds(pl.multiple_of(OWN * core, OWN), OWN)
    my_values = values_t.at[my_rows, pl.ds(0, CTX * ROWS)]
    remote(my_values, my_values, VALUE_PAIR, {"ctx": pair}).start()

    @pl.loop(0, CTX // 2)
    def _(r):
        source = lax.rem(me + CTX - 2 * r, CTX)
        block = keys.at[pl.ds(source * ROWS, ROWS)]
        pltpu.make_async_copy(block, block, key_recv.at[r]).wait()
        remote(block, block, KEY_PAIR, {"ctx": pair}).start()

    @pl.loop(1, CTX)
    def _(r):
        to = lax.rem(me + r, CTX)
        block = values_t.at[my_rows, pl.ds(pl.multiple_of(to * ROWS, ROWS), ROWS)]
        remote(block, home_in.at[me], HOME, {"ctx": to}).start()

    own_home = pltpu.make_async_copy(
        values_t.at[my_rows, pl.ds(pl.multiple_of(me * ROWS, ROWS), ROWS)], home_in.at[me], local.at[0]
    )
    own_home.start()

    wait_in(source_in, VALUE_PAIR)
    wait_in(keys.at[pl.ds(0, 16 * ROWS)], KEY_PAIR)

    def attend(u, start, blocks, clear):
        rows = pl.ds(pl.multiple_of(start, ROWS), blocks * ROWS)
        some_keys = jnp.concatenate([keys[rows], key_docs[rows]], axis=1)
        both = pl.ds(2 * u, 2)
        some_queries = jnp.concatenate([queries[both], query_docs[both]], axis=2)
        scores = nt_dot(some_keys, some_queries.reshape(2 * ROWS, 256))
        shape = ((blocks - clear) * ROWS, 2 * ROWS)
        at_key = lax.broadcasted_iota(jnp.int32, shape, 0) + (start + clear * ROWS)
        at_query = lax.broadcasted_iota(jnp.int32, shape, 1)
        at_query = jnp.where(at_query >= ROWS, at_query + ROWS, at_query) + (4 * u + core) * ROWS
        late = jnp.where(at_key <= at_query, scores[clear * ROWS :], MASKED)
        if clear:
            late = jnp.concatenate([scores[: clear * ROWS], late], axis=0)
        top = jnp.max(late, axis=0, keepdims=True)
        weights = jnp.exp2((late - top) * EXPONENT).astype(BF16)
        numerator = nn_dot(values_t[:, rows], weights)
        result = (numerator[0:64] * (1.0 / numerator[64:65])).astype(BF16)
        attn_t[2 * u] = result[:, :ROWS]
        attn_t[2 * u + 1] = result[:, ROWS:]

    def give(q):
        block = 2 * q + core

        @pl.when(q == mine)
        def _():
            pltpu.make_async_copy(attn_t.at[q], attn_in.at[mine], local.at[1]).start()

        @pl.when(q != mine)
        def _():
            remote(attn_t.at[q], attn_in.at[mine], ATTN, {"ctx": block}).start()

    @pl.loop(0, 8)
    def _(p):
        u = lax.rem(lax.div(mine + 1, 2) + 7 - p, 8)
        for at in range(2):
            block = queries.at[2 * u + at]
            arrived = query_recv.at[lax.rem(mine + 16 - 2 * u - at, 16)]
            pltpu.make_async_copy(block, block, arrived).wait()

        @pl.when(u < 2)
        def _():
            attend(u, 0, 8, 0)

        @pl.when((u >= 2) & (u < 4))
        def _():
            attend(u, 0, 16, 8)

        @pl.when(u >= 4)
        def _():
            attend(u, (4 * u + core) * ROWS - REACH, 19, 16)

        give(2 * u)
        give(2 * u + 1)

    wait_in(home_in.at[pl.ds(0, CTX - 1)], HOME)
    wait_in(attn_in.at[pl.ds(0, 15)], ATTN)

    own_home.wait()
    pltpu.make_async_copy(attn_t.at[mine], attn_in.at[mine], local.at[1]).wait()
    wait_out(squares.at[pl.ds(0, CH - 1)], SQUARES)
    wait_out(meta_in.at[pl.ds(0, CTX - 1)], META)
    wait_out(source_out.at[pl.ds(0, CTX - 1)], SOURCE)
    wait_out(gate_out.at[pl.ds(0, CTX - 1)], GATE)
    wait_out(queries.at[pl.ds(0, 15)], QUERY)
    wait_out(keys.at[pl.ds(0, 15 * ROWS)], KEY)
    wait_out(keys.at[pl.ds(0, 16 * ROWS)], KEY_PAIR)
    wait_out(source_in, VALUE_PAIR)
    wait_out(home_in.at[pl.ds(0, CTX - 1)], HOME)
    wait_out(attn_in.at[pl.ds(0, 15)], ATTN)


def turn(home_ref, attn_ref, hyena_out_ref, attn_out_ref):
    hyena_out_ref[...] = home_ref[...].astype(F32).T.astype(BF16)
    attn_out_ref[...] = attn_ref[...].astype(F32).T.astype(BF16)


def per_device(
    hyena_query,
    hyena_key,
    token_ids,
    embed_table,
    norm_gain,
    hyena_filter,
    attn_query,
    attn_key,
    document_ids,
):
    vmem = pl.BlockSpec(memory_space=pltpu.VMEM)
    hbm = pl.BlockSpec(memory_space=pltpu.HBM)
    shape = jax.ShapeDtypeStruct((ROWS, WIDTH), BF16)
    sent = pl.pallas_call(
        kernel,
        out_shape=(
            jax.ShapeDtypeStruct((CTX, OWN, ROWS), BF16),
            jax.ShapeDtypeStruct((16, 64, ROWS), BF16),
        ),
        in_specs=[hbm] * 9,
        out_specs=(hbm, hbm),
        scratch_shapes=[
            pltpu.VMEM((1, ROWS), jnp.int32),
            pltpu.VMEM((1, ROWS), jnp.int32),
            pltpu.VMEM((VOCAB, WIDTH), BF16),
            pltpu.VMEM((1, WIDTH), F32),
            pltpu.VMEM((ROWS, WIDTH), BF16),
            pltpu.VMEM((ROWS, WIDTH), BF16),
            pltpu.VMEM((64, ROWS), F32),
            pltpu.VMEM((CH, 8, VOCAB), F32),
            pltpu.VMEM((1, CTX * ROWS), jnp.int32),
            pltpu.VMEM((1, CTX * ROWS), F32),
            pltpu.VMEM((2, 256, 256), BF16),
            pltpu.VMEM((CTX, 4, ROWS), F32),
            pltpu.VMEM((CTX, 4, ROWS), F32),
            pltpu.VMEM((CTX, OWN, ROWS), BF16),
            pltpu.VMEM((CTX, OWN, ROWS), BF16),
            pltpu.VMEM((CTX, OWN, ROWS), BF16),
            pltpu.VMEM((CTX, OWN, ROWS), BF16),
            pltpu.VMEM((2, 16, 256, 256), BF16),
            pltpu.VMEM((2, 256, 256), F32),
            pltpu.VMEM((80, CTX * ROWS), BF16),
            pltpu.VMEM((CTX * ROWS, 128), BF16),
            pltpu.VMEM((CTX * ROWS, 128), BF16),
            pltpu.VMEM((16, ROWS, HEAD_DIM), BF16),
            pltpu.VMEM((16, ROWS, HEAD_DIM), BF16),
            pltpu.VMEM((16, 64, ROWS), BF16),
            pltpu.SemaphoreType.DMA((10,)),
            pltpu.SemaphoreType.DMA((10,)),
            pltpu.SemaphoreType.DMA((7,)),
            pltpu.SemaphoreType.DMA((CTX // 2,)),
            pltpu.SemaphoreType.DMA((CTX // 2,)),
        ],
        compiler_params=pltpu.CompilerParams(
            collective_id=0, has_side_effects=True, vmem_limit_bytes=60 * 1024 * 1024
        ),
    )(
        token_ids.reshape(1, ROWS),
        document_ids.reshape(1, ROWS),
        embed_table,
        norm_gain.reshape(1, WIDTH),
        hyena_query,
        hyena_key,
        hyena_filter.T,
        attn_query,
        attn_key,
    )
    return pl.pallas_call(
        turn,
        out_shape=(shape, shape),
        in_specs=[vmem] * 2,
        out_specs=(vmem, vmem),
    )(*(part.reshape(WIDTH, ROWS) for part in sent))


def solution(mesh):
    placed = (
        P("ctx", "ch"),
        P("ctx", "ch"),
        P("ctx"),
        P(None, "ch"),
        P("ch"),
        P("ctx", "ch"),
        P("ctx", "ch"),
        P("ctx", "ch"),
        P("ctx"),
    )
    return jax.shard_map(
        per_device,
        mesh=mesh,
        in_specs=placed,
        out_specs=(P("ctx", "ch"), P("ctx", "ch")),
        check_vma=False,
    )
```

```python
import functools
import math

import jax
import jax.numpy as jnp
from jax import lax
from jax.experimental import pallas as pl
from jax.experimental.pallas import tpu as pltpu
from jax.sharding import PartitionSpec as P

MESH = pl.DeviceIdType.MESH
F32 = jnp.float32
BF16 = jnp.bfloat16

CTX = 32
CH = 4
ROWS = 128
WIDTH = 1024
VOCAB = 512
CHANNELS = 4096
OWN = 32
GROUP = 16
HEAD_DIM = 128
REACH = 2048
EPSILON = 1e-06
MASKED = -1e30
SAME = 8192.0
EXPONENT = HEAD_DIM**-0.5 * math.log2(math.e)

META, SOURCE, GATE, QUERY, KEY, KEY_PAIR, VALUE_PAIR, HOME, ATTN, SQUARES = range(10)


def nt_dot(a, b):
    return lax.dot_general(a, b, (((1,), (1,)), ((), ())), preferred_element_type=F32)


def nn_dot(a, b):
    return jnp.dot(a, b, preferred_element_type=F32)


def halves(value):
    high = value.astype(BF16)
    return high, (value - high.astype(F32)).astype(BF16)


def kernel(
    ids_hbm,
    docs_hbm,
    table_hbm,
    gain_hbm,
    gate_hbm,
    key_hbm,
    filter_hbm,
    attn_query_ref,
    attn_key_ref,
    home_in,
    attn_in,
    ids_ref,
    docs_ref,
    table_ref,
    gain_ref,
    gate_ref,
    key_ref,
    filter_ref,
    squares,
    ids_row,
    scales,
    signals,
    meta_out,
    meta_in,
    source_out,
    source_in,
    gate_out,
    gate_in,
    toeplitz,
    sums,
    values_t,
    keys,
    key_docs,
    queries,
    query_docs,
    attn_t,
    send,
    recv,
    local,
    key_recv,
    query_recv,
):
    me = lax.axis_index("ctx")
    my_ch = lax.axis_index("ch")
    core = lax.rem(me, 2)
    mine = lax.div(me, 2)
    pair = me + 1 - 2 * core

    def remote(src, dst, kind, to, arrived=None):
        return pltpu.make_async_remote_copy(
            src_ref=src,
            dst_ref=dst,
            send_sem=send.at[kind],
            recv_sem=recv.at[kind] if arrived is None else arrived,
            device_id=to,
            device_id_type=MESH,
        )

    def wait_in(ref, kind):
        pltpu.make_async_copy(ref, ref, recv.at[kind]).wait()

    def wait_out(ref, kind):
        pltpu.make_async_copy(ref, ref, send.at[kind]).wait()

    loads = [
        pltpu.make_async_copy(src, dst, local.at[at])
        for at, (src, dst) in enumerate(
            (
                (table_hbm, table_ref),
                (filter_hbm, filter_ref),
                (docs_hbm, docs_ref),
                (ids_hbm, ids_ref),
                (key_hbm, key_ref),
                (gain_hbm, gain_ref),
                (gate_hbm, gate_ref),
            )
        )
    ]
    for load in loads:
        load.start()

    my_keys = keys.at[pl.ds(me * ROWS, ROWS)]
    my_queries = queries.at[mine]
    my_head = pl.ds(pl.multiple_of(lax.div(me, 4) * HEAD_DIM, HEAD_DIM), HEAD_DIM)
    pltpu.make_async_copy(attn_key_ref.at[:, my_head], my_keys, key_recv.at[0]).start()
    pltpu.make_async_copy(attn_query_ref.at[:, my_head], my_queries, query_recv.at[0]).start()

    barrier = pltpu.get_barrier_semaphore()

    @pl.loop(1, CTX)
    def _(r):
        pl.semaphore_signal(
            barrier, inc=1, device_id={"ctx": lax.rem(me + r, CTX)}, device_id_type=MESH
        )

    for r in range(1, CH):
        pl.semaphore_signal(
            barrier, inc=1, device_id={"ch": lax.rem(my_ch + r, CH)}, device_id_type=MESH
        )

    for load in loads[:6]:
        load.wait()

    taps = filter_ref[...]
    docs = docs_ref[...].astype(F32)
    ids = ids_ref[...].astype(F32)
    for d in range(CTX):
        meta_out[d] = jnp.concatenate([taps[2 * d : 2 * d + 2], docs, ids], axis=0)
    meta_in[me] = meta_out[me]

    one_hot_t = (lax.broadcasted_iota(jnp.int32, (VOCAB, ROWS), 0) == ids_ref[...]).astype(F32)
    picked = nn_dot(one_hot_t.T.astype(BF16), table_ref[...])
    product = picked * key_ref[...].astype(F32) * gain_ref[...]
    source_out[...] = product.T.astype(BF16).reshape(CTX, OWN, ROWS)
    source_in[me] = source_out[me]

    by_lane = jnp.zeros((VOCAB, 128), F32)
    for tile in range(WIDTH // 128):
        part = table_ref[:, tile * 128 : (tile + 1) * 128].astype(F32)
        by_lane = by_lane + part * part
    high, low = halves(by_lane)
    ones = jnp.ones((8, 128), BF16)
    squares[my_ch] = nt_dot(ones, high) + nt_dot(ones, low)

    loads[6].wait()
    gate_out[...] = gate_ref[...].astype(F32).T.astype(BF16).reshape(CTX, OWN, ROWS)
    gate_in[me] = gate_out[me]

    values_t[64:80, :] = jnp.ones((16, CTX * ROWS), BF16)

    pl.semaphore_wait(barrier, CTX - 1 + CH - 1)

    for r in range(1, CH):
        to = lax.rem(my_ch + r, CH)
        remote(squares.at[my_ch], squares.at[my_ch], SQUARES, {"ch": to}).start()

    @pl.loop(1, CTX)
    def _(r):
        to = lax.rem(me + r, CTX)
        remote(source_out.at[to], source_in.at[me], SOURCE, {"ctx": to}).start()

    @pl.loop(1, CTX)
    def _(r):
        to = lax.rem(me + r, CTX)
        remote(meta_out.at[to], meta_in.at[me], META, {"ctx": to}).start()

    @pl.loop(1, CTX)
    def _(r):
        to = lax.rem(me + r, CTX)
        remote(gate_out.at[to], gate_in.at[me], GATE, {"ctx": to}).start()

    @pl.loop(1, CTX // 2)
    def _(r):
        to = lax.rem(me + 2 * r, CTX)
        head = pl.ds(pl.multiple_of(lax.div(to, 4) * HEAD_DIM, HEAD_DIM), HEAD_DIM)
        remote(attn_key_ref.at[:, head], my_keys, KEY, {"ctx": to}, key_recv.at[r]).start()

    @pl.loop(1, CTX // 2)
    def _(r):
        to = lax.rem(me + 2 * r, CTX)
        head = pl.ds(pl.multiple_of(lax.div(to, 4) * HEAD_DIM, HEAD_DIM), HEAD_DIM)
        remote(
            attn_query_ref.at[:, head], my_queries, QUERY, {"ctx": to}, query_recv.at[r]
        ).start()

    wait_in(meta_in.at[pl.ds(0, CTX - 1)], META)
    down = lax.broadcasted_iota(jnp.int32, (ROWS, ROWS), 0)
    right = lax.broadcasted_iota(jnp.int32, (ROWS, ROWS), 1)
    upper = right >= down

    def turned(n, g):
        row = jnp.broadcast_to(meta_in[n, g : g + 1, :], (ROWS, ROWS))
        return pltpu.roll(row, 0, 1, stride=1, stride_axis=0)

    for g in range(2):

        def build(k, carry):
            before, block_before = carry
            first = turned(2 * k, g)
            second = turned(2 * k + 1, g)
            block = jnp.where(upper, first, before).astype(BF16)
            block_next = jnp.where(upper, second, first).astype(BF16)
            toeplitz[g, k, 0:128, 0:128] = block
            toeplitz[g, k, 128:256, 128:256] = block
            toeplitz[g, k, 0:128, 128:256] = block_next
            toeplitz[g, k, 128:256, 0:128] = block_before
            return second, block_next

        lax.fori_loop(
            0, 16, build, (jnp.zeros((ROWS, ROWS), F32), jnp.zeros((ROWS, ROWS), BF16))
        )

    @pl.loop(0, CTX)
    def _(j):
        which = down.astype(F32) == meta_in[j, 2:3, :]
        key_docs[pl.ds(pl.multiple_of(j * ROWS, ROWS), ROWS)] = (
            which.astype(F32).T.astype(BF16)
        )

    @pl.loop(0, 16)
    def _(q):
        rows = pl.ds(pl.multiple_of((2 * q + core) * ROWS, ROWS), ROWS)
        query_docs[q] = (key_docs[rows].astype(F32) * SAME).astype(BF16)

    for j in range(CTX):
        ids_row[:, j * ROWS : (j + 1) * ROWS] = meta_in[j, 3:4, :].astype(jnp.int32)
    wait_in(squares.at[pl.ds(0, CH - 1)], SQUARES)
    total = (squares[0] + squares[1] + squares[2] + squares[3])[0:1]
    low_digit = lax.broadcasted_iota(jnp.int32, (16, VOCAB), 0)
    token = lax.broadcasted_iota(jnp.int32, (16, VOCAB), 1)
    high, low = halves(jnp.where(lax.rem(token, 16) == low_digit, total, 0.0))
    high_digit = lax.broadcasted_iota(jnp.int32, (32, VOCAB), 0)
    token = lax.broadcasted_iota(jnp.int32, (32, VOCAB), 1)
    gather = (lax.div(token, 16) == high_digit).astype(F32).astype(BF16)
    high, low = halves(nt_dot(high, gather) + nt_dot(low, gather))
    digits = lax.div(ids_row[...], 16)
    chosen = lax.broadcasted_iota(jnp.int32, (32, CTX * ROWS), 0) == digits
    chosen = chosen.astype(F32).astype(BF16)
    choices = nn_dot(high, chosen) + nn_dot(low, chosen)
    digits = lax.rem(ids_row[...], 16)
    chosen = lax.broadcasted_iota(jnp.int32, (16, CTX * ROWS), 0) == digits
    square = jnp.sum(jnp.where(chosen, choices, 0.0), axis=0, keepdims=True)
    scales[...] = lax.rsqrt(square * (1.0 / CHANNELS) + EPSILON)

    wait_in(source_in.at[pl.ds(0, CTX - 1)], SOURCE)
    for j in range(CTX):
        scaled = source_in[j].astype(F32) * scales[:, j * ROWS : (j + 1) * ROWS]
        scaled = scaled.astype(BF16)
        lanes = slice(j % 2 * ROWS, (j % 2 + 1) * ROWS)
        for g in range(2):
            signals[g, j // 2 * GROUP : (j // 2 + 1) * GROUP, lanes] = scaled[
                g * GROUP : (g + 1) * GROUP
            ]
    for g in range(2):
        signal = signals[g]
        sums[g] = nn_dot(signal, toeplitz[g, 0])
        for k in range(1, 16):
            sums[g, 16 * k :] += nn_dot(signal[: 256 - 16 * k], toeplitz[g, k])

    wait_in(gate_in.at[pl.ds(0, CTX - 1)], GATE)
    for g in range(2):
        own = slice(g * GROUP, (g + 1) * GROUP)
        rows = pl.ds(pl.multiple_of(OWN * core + GROUP * g, GROUP), GROUP)
        for j in range(16):
            gate = jnp.concatenate([gate_in[2 * j, own, :], gate_in[2 * j + 1, own, :]], axis=1)
            gated = sums[g, 16 * j : 16 * (j + 1)] * gate.astype(F32)
            values_t[rows, 256 * j : 256 * (j + 1)] = gated.astype(BF16)

    my_rows = pl.ds(pl.multiple_of(OWN * core, OWN), OWN)
    my_values = values_t.at[my_rows, pl.ds(0, CTX * ROWS)]
    remote(my_values, my_values, VALUE_PAIR, {"ctx": pair}).start()

    @pl.loop(0, CTX // 2)
    def _(r):
        source = lax.rem(me + CTX - 2 * r, CTX)
        block = keys.at[pl.ds(source * ROWS, ROWS)]
        pltpu.make_async_copy(block, block, key_recv.at[r]).wait()
        remote(block, block, KEY_PAIR, {"ctx": pair}).start()

    @pl.loop(1, CTX)
    def _(r):
        to = lax.rem(me + r, CTX)
        block = values_t.at[my_rows, pl.ds(pl.multiple_of(to * ROWS, ROWS), ROWS)]
        remote(block, home_in.at[me], HOME, {"ctx": to}).start()

    own_home = pltpu.make_async_copy(
        values_t.at[my_rows, pl.ds(pl.multiple_of(me * ROWS, ROWS), ROWS)], home_in.at[me], local.at[0]
    )
    own_home.start()

    wait_in(source_in, VALUE_PAIR)
    wait_in(keys.at[pl.ds(0, 16 * ROWS)], KEY_PAIR)

    def attend(u, start, blocks, clear):
        rows = pl.ds(pl.multiple_of(start, ROWS), blocks * ROWS)
        some_keys = jnp.concatenate([keys[rows], key_docs[rows]], axis=1)
        both = pl.ds(2 * u, 2)
        some_queries = jnp.concatenate([queries[both], query_docs[both]], axis=2)
        scores = nt_dot(some_keys, some_queries.reshape(2 * ROWS, 256))
        shape = ((blocks - clear) * ROWS, 2 * ROWS)
        at_key = lax.broadcasted_iota(jnp.int32, shape, 0) + (start + clear * ROWS)
        at_query = lax.broadcasted_iota(jnp.int32, shape, 1)
        at_query = jnp.where(at_query >= ROWS, at_query + ROWS, at_query) + (4 * u + core) * ROWS
        late = jnp.where(at_key <= at_query, scores[clear * ROWS :], MASKED)
        if clear:
            late = jnp.concatenate([scores[: clear * ROWS], late], axis=0)
        top = jnp.max(late, axis=0, keepdims=True)
        weights = jnp.exp2((late - top) * EXPONENT).astype(BF16)
        numerator = nn_dot(values_t[:, rows], weights)
        result = (numerator[0:64] * (1.0 / numerator[64:65])).astype(BF16)
        attn_t[2 * u] = result[:, :ROWS]
        attn_t[2 * u + 1] = result[:, ROWS:]

    def give(q):
        block = 2 * q + core

        @pl.when(q == mine)
        def _():
            pltpu.make_async_copy(attn_t.at[q], attn_in.at[mine], local.at[1]).start()

        @pl.when(q != mine)
        def _():
            remote(attn_t.at[q], attn_in.at[mine], ATTN, {"ctx": block}).start()

    @pl.loop(0, 8)
    def _(p):
        u = lax.rem(lax.div(mine + 1, 2) + 7 - p, 8)
        for at in range(2):
            block = queries.at[2 * u + at]
            arrived = query_recv.at[lax.rem(mine + 16 - 2 * u - at, 16)]
            pltpu.make_async_copy(block, block, arrived).wait()

        @pl.when(u < 2)
        def _():
            attend(u, 0, 8, 0)

        @pl.when((u >= 2) & (u < 4))
        def _():
            attend(u, 0, 16, 8)

        @pl.when(u >= 4)
        def _():
            attend(u, (4 * u + core) * ROWS - REACH, 19, 16)

        give(2 * u)
        give(2 * u + 1)

    wait_in(home_in.at[pl.ds(0, CTX - 1)], HOME)
    wait_in(attn_in.at[pl.ds(0, 15)], ATTN)

    own_home.wait()
    pltpu.make_async_copy(attn_t.at[mine], attn_in.at[mine], local.at[1]).wait()
    wait_out(squares.at[pl.ds(0, CH - 1)], SQUARES)
    wait_out(meta_in.at[pl.ds(0, CTX - 1)], META)
    wait_out(source_out.at[pl.ds(0, CTX - 1)], SOURCE)
    wait_out(gate_out.at[pl.ds(0, CTX - 1)], GATE)
    wait_out(queries.at[pl.ds(0, 15)], QUERY)
    wait_out(keys.at[pl.ds(0, 15 * ROWS)], KEY)
    wait_out(keys.at[pl.ds(0, 16 * ROWS)], KEY_PAIR)
    wait_out(source_in, VALUE_PAIR)
    wait_out(home_in.at[pl.ds(0, CTX - 1)], HOME)
    wait_out(attn_in.at[pl.ds(0, 15)], ATTN)


def turn(home_ref, attn_ref, hyena_out_ref, attn_out_ref):
    hyena_out_ref[...] = home_ref[...].astype(F32).T.astype(BF16)
    attn_out_ref[...] = attn_ref[...].astype(F32).T.astype(BF16)


def per_device(
    hyena_query,
    hyena_key,
    token_ids,
    embed_table,
    norm_gain,
    hyena_filter,
    attn_query,
    attn_key,
    document_ids,
):
    vmem = pl.BlockSpec(memory_space=pltpu.VMEM)
    hbm = pl.BlockSpec(memory_space=pltpu.HBM)
    shape = jax.ShapeDtypeStruct((ROWS, WIDTH), BF16)
    sent = pl.pallas_call(
        kernel,
        out_shape=(
            jax.ShapeDtypeStruct((CTX, OWN, ROWS), BF16),
            jax.ShapeDtypeStruct((16, 64, ROWS), BF16),
        ),
        in_specs=[hbm] * 9,
        out_specs=(hbm, hbm),
        scratch_shapes=[
            pltpu.VMEM((1, ROWS), jnp.int32),
            pltpu.VMEM((1, ROWS), jnp.int32),
            pltpu.VMEM((VOCAB, WIDTH), BF16),
            pltpu.VMEM((1, WIDTH), F32),
            pltpu.VMEM((ROWS, WIDTH), BF16),
            pltpu.VMEM((ROWS, WIDTH), BF16),
            pltpu.VMEM((64, ROWS), F32),
            pltpu.VMEM((CH, 8, VOCAB), F32),
            pltpu.VMEM((1, CTX * ROWS), jnp.int32),
            pltpu.VMEM((1, CTX * ROWS), F32),
            pltpu.VMEM((2, 256, 256), BF16),
            pltpu.VMEM((CTX, 4, ROWS), F32),
            pltpu.VMEM((CTX, 4, ROWS), F32),
            pltpu.VMEM((CTX, OWN, ROWS), BF16),
            pltpu.VMEM((CTX, OWN, ROWS), BF16),
            pltpu.VMEM((CTX, OWN, ROWS), BF16),
            pltpu.VMEM((CTX, OWN, ROWS), BF16),
            pltpu.VMEM((2, 16, 256, 256), BF16),
            pltpu.VMEM((2, 256, 256), F32),
            pltpu.VMEM((80, CTX * ROWS), BF16),
            pltpu.VMEM((CTX * ROWS, 128), BF16),
            pltpu.VMEM((CTX * ROWS, 128), BF16),
            pltpu.VMEM((16, ROWS, HEAD_DIM), BF16),
            pltpu.VMEM((16, ROWS, HEAD_DIM), BF16),
            pltpu.VMEM((16, 64, ROWS), BF16),
            pltpu.SemaphoreType.DMA((10,)),
            pltpu.SemaphoreType.DMA((10,)),
            pltpu.SemaphoreType.DMA((7,)),
            pltpu.SemaphoreType.DMA((CTX // 2,)),
            pltpu.SemaphoreType.DMA((CTX // 2,)),
        ],
        compiler_params=pltpu.CompilerParams(
            collective_id=0, has_side_effects=True, vmem_limit_bytes=60 * 1024 * 1024
        ),
    )(
        token_ids.reshape(1, ROWS),
        document_ids.reshape(1, ROWS),
        embed_table,
        norm_gain.reshape(1, WIDTH),
        hyena_query,
        hyena_key,
        hyena_filter.T,
        attn_query,
        attn_key,
    )
    return pl.pallas_call(
        turn,
        out_shape=(shape, shape),
        in_specs=[vmem] * 2,
        out_specs=(vmem, vmem),
    )(*(part.reshape(WIDTH, ROWS) for part in sent))


def solution(mesh):
    placed = (
        P("ctx", "ch"),
        P("ctx", "ch"),
        P("ctx"),
        P(None, "ch"),
        P("ch"),
        P("ctx", "ch"),
        P("ctx", "ch"),
        P("ctx", "ch"),
        P("ctx"),
    )
    return jax.shard_map(
        per_device,
        mesh=mesh,
        in_specs=placed,
        out_specs=(P("ctx", "ch"), P("ctx", "ch")),
        check_vma=False,
    )
```

```python
import functools
import math

import jax
import jax.numpy as jnp
from jax import lax
from jax.experimental import pallas as pl
from jax.experimental.pallas import tpu as pltpu
from jax.sharding import PartitionSpec as P

MESH = pl.DeviceIdType.MESH
F32 = jnp.float32
BF16 = jnp.bfloat16

CTX = 32
CH = 4
ROWS = 128
WIDTH = 1024
VOCAB = 512
CHANNELS = 4096
OWN = 32
GROUP = 16
HEAD_DIM = 128
REACH = 2048
EPSILON = 1e-06
MASKED = -1e30
SAME = 8192.0
EXPONENT = HEAD_DIM**-0.5 * math.log2(math.e)

META, SOURCE, GATE, QUERY, KEY, KEY_PAIR, VALUE_PAIR, HOME, ATTN, SQUARES = range(10)


def nt_dot(a, b):
    return lax.dot_general(a, b, (((1,), (1,)), ((), ())), preferred_element_type=F32)


def nn_dot(a, b):
    return jnp.dot(a, b, preferred_element_type=F32)


def halves(value):
    high = value.astype(BF16)
    return high, (value - high.astype(F32)).astype(BF16)


def kernel(
    ids_hbm,
    docs_hbm,
    table_hbm,
    gain_hbm,
    gate_hbm,
    key_hbm,
    filter_hbm,
    attn_query_ref,
    attn_key_ref,
    home_in,
    attn_in,
    ids_ref,
    docs_ref,
    table_ref,
    gain_ref,
    gate_ref,
    key_ref,
    filter_ref,
    squares,
    ids_row,
    scales,
    signals,
    meta_out,
    meta_in,
    source_out,
    source_in,
    gate_out,
    gate_in,
    toeplitz,
    sums,
    values_t,
    keys,
    key_docs,
    queries,
    query_docs,
    attn_t,
    send,
    recv,
    local,
    key_recv,
    query_recv,
):
    me = lax.axis_index("ctx")
    my_ch = lax.axis_index("ch")
    core = lax.rem(me, 2)
    mine = lax.div(me, 2)
    pair = me + 1 - 2 * core

    def remote(src, dst, kind, to, arrived=None):
        return pltpu.make_async_remote_copy(
            src_ref=src,
            dst_ref=dst,
            send_sem=send.at[kind],
            recv_sem=recv.at[kind] if arrived is None else arrived,
            device_id=to,
            device_id_type=MESH,
        )

    def wait_in(ref, kind):
        pltpu.make_async_copy(ref, ref, recv.at[kind]).wait()

    def wait_out(ref, kind):
        pltpu.make_async_copy(ref, ref, send.at[kind]).wait()

    loads = [
        pltpu.make_async_copy(src, dst, local.at[at])
        for at, (src, dst) in enumerate(
            (
                (table_hbm, table_ref),
                (filter_hbm, filter_ref),
                (docs_hbm, docs_ref),
                (ids_hbm, ids_ref),
                (key_hbm, key_ref),
                (gain_hbm, gain_ref),
                (gate_hbm, gate_ref),
            )
        )
    ]
    for load in loads:
        load.start()

    my_keys = keys.at[pl.ds(me * ROWS, ROWS)]
    my_queries = queries.at[mine]
    my_head = pl.ds(pl.multiple_of(lax.div(me, 4) * HEAD_DIM, HEAD_DIM), HEAD_DIM)
    pltpu.make_async_copy(attn_key_ref.at[:, my_head], my_keys, key_recv.at[0]).start()
    pltpu.make_async_copy(attn_query_ref.at[:, my_head], my_queries, query_recv.at[0]).start()

    barrier = pltpu.get_barrier_semaphore()

    @pl.loop(1, CTX)
    def _(r):
        pl.semaphore_signal(
            barrier, inc=1, device_id={"ctx": lax.rem(me + r, CTX)}, device_id_type=MESH
        )

    for r in range(1, CH):
        pl.semaphore_signal(
            barrier, inc=1, device_id={"ch": lax.rem(my_ch + r, CH)}, device_id_type=MESH
        )

    for load in loads[:6]:
        load.wait()

    taps = filter_ref[...]
    docs = docs_ref[...].astype(F32)
    ids = ids_ref[...].astype(F32)
    for d in range(CTX):
        meta_out[d] = jnp.concatenate([taps[2 * d : 2 * d + 2], docs, ids], axis=0)
    meta_in[me] = meta_out[me]

    one_hot_t = (lax.broadcasted_iota(jnp.int32, (VOCAB, ROWS), 0) == ids_ref[...]).astype(F32)
    picked = nn_dot(one_hot_t.T.astype(BF16), table_ref[...])
    product = picked * key_ref[...].astype(F32) * gain_ref[...]
    source_out[...] = product.T.astype(BF16).reshape(CTX, OWN, ROWS)
    source_in[me] = source_out[me]

    by_lane = jnp.zeros((VOCAB, 128), F32)
    for tile in range(WIDTH // 128):
        part = table_ref[:, tile * 128 : (tile + 1) * 128].astype(F32)
        by_lane = by_lane + part * part
    high, low = halves(by_lane)
    ones = jnp.ones((8, 128), BF16)
    squares[my_ch] = nt_dot(ones, high) + nt_dot(ones, low)

    loads[6].wait()
    gate_out[...] = gate_ref[...].astype(F32).T.astype(BF16).reshape(CTX, OWN, ROWS)
    gate_in[me] = gate_out[me]

    values_t[64:80, :] = jnp.ones((16, CTX * ROWS), BF16)

    pl.semaphore_wait(barrier, CTX - 1 + CH - 1)

    for r in range(1, CH):
        to = lax.rem(my_ch + r, CH)
        remote(squares.at[my_ch], squares.at[my_ch], SQUARES, {"ch": to}).start()

    @pl.loop(1, CTX)
    def _(r):
        to = lax.rem(me + r, CTX)
        remote(source_out.at[to], source_in.at[me], SOURCE, {"ctx": to}).start()

    @pl.loop(1, CTX)
    def _(r):
        to = lax.rem(me + r, CTX)
        remote(meta_out.at[to], meta_in.at[me], META, {"ctx": to}).start()

    @pl.loop(1, CTX)
    def _(r):
        to = lax.rem(me + r, CTX)
        remote(gate_out.at[to], gate_in.at[me], GATE, {"ctx": to}).start()

    @pl.loop(1, CTX // 2)
    def _(r):
        to = lax.rem(me + 2 * r, CTX)
        head = pl.ds(pl.multiple_of(lax.div(to, 4) * HEAD_DIM, HEAD_DIM), HEAD_DIM)
        remote(attn_key_ref.at[:, head], my_keys, KEY, {"ctx": to}, key_recv.at[r]).start()

    @pl.loop(1, CTX // 2)
    def _(r):
        to = lax.rem(me + 2 * r, CTX)
        head = pl.ds(pl.multiple_of(lax.div(to, 4) * HEAD_DIM, HEAD_DIM), HEAD_DIM)
        remote(
            attn_query_ref.at[:, head], my_queries, QUERY, {"ctx": to}, query_recv.at[r]
        ).start()

    wait_in(meta_in.at[pl.ds(0, CTX - 1)], META)
    down = lax.broadcasted_iota(jnp.int32, (ROWS, ROWS), 0)
    right = lax.broadcasted_iota(jnp.int32, (ROWS, ROWS), 1)
    upper = right >= down

    def turned(n, g):
        row = jnp.broadcast_to(meta_in[n, g : g + 1, :], (ROWS, ROWS))
        return pltpu.roll(row, 0, 1, stride=1, stride_axis=0)

    for g in range(2):

        def build(k, carry):
            before, block_before = carry
            first = turned(2 * k, g)
            second = turned(2 * k + 1, g)
            block = jnp.where(upper, first, before).astype(BF16)
            block_next = jnp.where(upper, second, first).astype(BF16)
            toeplitz[g, k, 0:128, 0:128] = block
            toeplitz[g, k, 128:256, 128:256] = block
            toeplitz[g, k, 0:128, 128:256] = block_next
            toeplitz[g, k, 128:256, 0:128] = block_before
            return second, block_next

        lax.fori_loop(
            0, 16, build, (jnp.zeros((ROWS, ROWS), F32), jnp.zeros((ROWS, ROWS), BF16))
        )

    @pl.loop(0, CTX)
    def _(j):
        which = down.astype(F32) == meta_in[j, 2:3, :]
        key_docs[pl.ds(pl.multiple_of(j * ROWS, ROWS), ROWS)] = (
            which.astype(F32).T.astype(BF16)
        )

    @pl.loop(0, 16)
    def _(q):
        rows = pl.ds(pl.multiple_of((2 * q + core) * ROWS, ROWS), ROWS)
        query_docs[q] = (key_docs[rows].astype(F32) * SAME).astype(BF16)

    for j in range(CTX):
        ids_row[:, j * ROWS : (j + 1) * ROWS] = meta_in[j, 3:4, :].astype(jnp.int32)
    wait_in(squares.at[pl.ds(0, CH - 1)], SQUARES)
    total = (squares[0] + squares[1] + squares[2] + squares[3])[0:1]
    low_digit = lax.broadcasted_iota(jnp.int32, (16, VOCAB), 0)
    token = lax.broadcasted_iota(jnp.int32, (16, VOCAB), 1)
    high, low = halves(jnp.where(lax.rem(token, 16) == low_digit, total, 0.0))
    high_digit = lax.broadcasted_iota(jnp.int32, (32, VOCAB), 0)
    token = lax.broadcasted_iota(jnp.int32, (32, VOCAB), 1)
    gather = (lax.div(token, 16) == high_digit).astype(F32).astype(BF16)
    high, low = halves(nt_dot(high, gather) + nt_dot(low, gather))
    digits = lax.div(ids_row[...], 16)
    chosen = lax.broadcasted_iota(jnp.int32, (32, CTX * ROWS), 0) == digits
    chosen = chosen.astype(F32).astype(BF16)
    choices = nn_dot(high, chosen) + nn_dot(low, chosen)
    digits = lax.rem(ids_row[...], 16)
    chosen = lax.broadcasted_iota(jnp.int32, (16, CTX * ROWS), 0) == digits
    square = jnp.sum(jnp.where(chosen, choices, 0.0), axis=0, keepdims=True)
    scales[...] = lax.rsqrt(square * (1.0 / CHANNELS) + EPSILON)

    wait_in(source_in.at[pl.ds(0, CTX - 1)], SOURCE)
    for j in range(CTX):
        scaled = source_in[j].astype(F32) * scales[:, j * ROWS : (j + 1) * ROWS]
        scaled = scaled.astype(BF16)
        lanes = slice(j % 2 * ROWS, (j % 2 + 1) * ROWS)
        for g in range(2):
            signals[g, j // 2 * GROUP : (j // 2 + 1) * GROUP, lanes] = scaled[
                g * GROUP : (g + 1) * GROUP
            ]
    for g in range(2):
        signal = signals[g]
        sums[g] = nn_dot(signal, toeplitz[g, 0])
        for k in range(1, 16):
            sums[g, 16 * k :] += nn_dot(signal[: 256 - 16 * k], toeplitz[g, k])

    wait_in(gate_in.at[pl.ds(0, CTX - 1)], GATE)
    for g in range(2):
        own = slice(g * GROUP, (g + 1) * GROUP)
        rows = pl.ds(pl.multiple_of(OWN * core + GROUP * g, GROUP), GROUP)
        for j in range(16):
            gate = jnp.concatenate([gate_in[2 * j, own, :], gate_in[2 * j + 1, own, :]], axis=1)
            gated = sums[g, 16 * j : 16 * (j + 1)] * gate.astype(F32)
            values_t[rows, 256 * j : 256 * (j + 1)] = gated.astype(BF16)

    my_rows = pl.ds(pl.multiple_of(OWN * core, OWN), OWN)
    my_values = values_t.at[my_rows, pl.ds(0, CTX * ROWS)]
    remote(my_values, my_values, VALUE_PAIR, {"ctx": pair}).start()

    @pl.loop(0, CTX // 2)
    def _(r):
        source = lax.rem(me + CTX - 2 * r, CTX)
        block = keys.at[pl.ds(source * ROWS, ROWS)]
        pltpu.make_async_copy(block, block, key_recv.at[r]).wait()
        remote(block, block, KEY_PAIR, {"ctx": pair}).start()

    @pl.loop(1, CTX)
    def _(r):
        to = lax.rem(me + r, CTX)
        block = values_t.at[my_rows, pl.ds(pl.multiple_of(to * ROWS, ROWS), ROWS)]
        remote(block, home_in.at[me], HOME, {"ctx": to}).start()

    own_home = pltpu.make_async_copy(
        values_t.at[my_rows, pl.ds(pl.multiple_of(me * ROWS, ROWS), ROWS)], home_in.at[me], local.at[0]
    )
    own_home.start()

    wait_in(source_in, VALUE_PAIR)
    wait_in(keys.at[pl.ds(0, 16 * ROWS)], KEY_PAIR)

    def attend(u, start, blocks, clear):
        rows = pl.ds(pl.multiple_of(start, ROWS), blocks * ROWS)
        some_keys = jnp.concatenate([keys[rows], key_docs[rows]], axis=1)
        both = pl.ds(2 * u, 2)
        some_queries = jnp.concatenate([queries[both], query_docs[both]], axis=2)
        scores = nt_dot(some_keys, some_queries.reshape(2 * ROWS, 256))
        shape = ((blocks - clear) * ROWS, 2 * ROWS)
        at_key = lax.broadcasted_iota(jnp.int32, shape, 0) + (start + clear * ROWS)
        at_query = lax.broadcasted_iota(jnp.int32, shape, 1)
        at_query = jnp.where(at_query >= ROWS, at_query + ROWS, at_query) + (4 * u + core) * ROWS
        late = jnp.where(at_key <= at_query, scores[clear * ROWS :], MASKED)
        if clear:
            late = jnp.concatenate([scores[: clear * ROWS], late], axis=0)
        top = jnp.max(late, axis=0, keepdims=True)
        weights = jnp.exp2((late - top) * EXPONENT).astype(BF16)
        numerator = nn_dot(values_t[:, rows], weights)
        result = (numerator[0:64] * (1.0 / numerator[64:65])).astype(BF16)
        attn_t[2 * u] = result[:, :ROWS]
        attn_t[2 * u + 1] = result[:, ROWS:]

    def give(q):
        block = 2 * q + core

        @pl.when(q == mine)
        def _():
            pltpu.make_async_copy(attn_t.at[q], attn_in.at[mine], local.at[1]).start()

        @pl.when(q != mine)
        def _():
            remote(attn_t.at[q], attn_in.at[mine], ATTN, {"ctx": block}).start()

    @pl.loop(0, 8)
    def _(p):
        u = lax.rem(lax.div(mine + 1, 2) + 7 - p, 8)
        for at in range(2):
            block = queries.at[2 * u + at]
            arrived = query_recv.at[lax.rem(mine + 16 - 2 * u - at, 16)]
            pltpu.make_async_copy(block, block, arrived).wait()

        for early in range(4):

            @pl.when(u == early)
            def _():
                attend(u, 0, 4 * early + 4, 4 * early)

        @pl.when(u >= 4)
        def _():
            attend(u, (4 * u + core) * ROWS - REACH, 19, 16)

        give(2 * u)
        give(2 * u + 1)

    wait_in(home_in.at[pl.ds(0, CTX - 1)], HOME)
    wait_in(attn_in.at[pl.ds(0, 15)], ATTN)

    own_home.wait()
    pltpu.make_async_copy(attn_t.at[mine], attn_in.at[mine], local.at[1]).wait()
    wait_out(squares.at[pl.ds(0, CH - 1)], SQUARES)
    wait_out(meta_in.at[pl.ds(0, CTX - 1)], META)
    wait_out(source_out.at[pl.ds(0, CTX - 1)], SOURCE)
    wait_out(gate_out.at[pl.ds(0, CTX - 1)], GATE)
    wait_out(queries.at[pl.ds(0, 15)], QUERY)
    wait_out(keys.at[pl.ds(0, 15 * ROWS)], KEY)
    wait_out(keys.at[pl.ds(0, 16 * ROWS)], KEY_PAIR)
    wait_out(source_in, VALUE_PAIR)
    wait_out(home_in.at[pl.ds(0, CTX - 1)], HOME)
    wait_out(attn_in.at[pl.ds(0, 15)], ATTN)


def turn(home_ref, attn_ref, hyena_out_ref, attn_out_ref):
    hyena_out_ref[...] = home_ref[...].T
    attn_out_ref[...] = attn_ref[...].T


def per_device(
    hyena_query,
    hyena_key,
    token_ids,
    embed_table,
    norm_gain,
    hyena_filter,
    attn_query,
    attn_key,
    document_ids,
):
    vmem = pl.BlockSpec(memory_space=pltpu.VMEM)
    hbm = pl.BlockSpec(memory_space=pltpu.HBM)
    shape = jax.ShapeDtypeStruct((ROWS, WIDTH), BF16)
    sent = pl.pallas_call(
        kernel,
        out_shape=(
            jax.ShapeDtypeStruct((CTX, OWN, ROWS), BF16),
            jax.ShapeDtypeStruct((16, 64, ROWS), BF16),
        ),
        in_specs=[hbm] * 9,
        out_specs=(hbm, hbm),
        scratch_shapes=[
            pltpu.VMEM((1, ROWS), jnp.int32),
            pltpu.VMEM((1, ROWS), jnp.int32),
            pltpu.VMEM((VOCAB, WIDTH), BF16),
            pltpu.VMEM((1, WIDTH), F32),
            pltpu.VMEM((ROWS, WIDTH), BF16),
            pltpu.VMEM((ROWS, WIDTH), BF16),
            pltpu.VMEM((64, ROWS), F32),
            pltpu.VMEM((CH, 8, VOCAB), F32),
            pltpu.VMEM((1, CTX * ROWS), jnp.int32),
            pltpu.VMEM((1, CTX * ROWS), F32),
            pltpu.VMEM((2, 256, 256), BF16),
            pltpu.VMEM((CTX, 4, ROWS), F32),
            pltpu.VMEM((CTX, 4, ROWS), F32),
            pltpu.VMEM((CTX, OWN, ROWS), BF16),
            pltpu.VMEM((CTX, OWN, ROWS), BF16),
            pltpu.VMEM((CTX, OWN, ROWS), BF16),
            pltpu.VMEM((CTX, OWN, ROWS), BF16),
            pltpu.VMEM((2, 16, 256, 256), BF16),
            pltpu.VMEM((2, 256, 256), F32),
            pltpu.VMEM((80, CTX * ROWS), BF16),
            pltpu.VMEM((CTX * ROWS, 128), BF16),
            pltpu.VMEM((CTX * ROWS, 128), BF16),
            pltpu.VMEM((16, ROWS, HEAD_DIM), BF16),
            pltpu.VMEM((16, ROWS, HEAD_DIM), BF16),
            pltpu.VMEM((16, 64, ROWS), BF16),
            pltpu.SemaphoreType.DMA((10,)),
            pltpu.SemaphoreType.DMA((10,)),
            pltpu.SemaphoreType.DMA((7,)),
            pltpu.SemaphoreType.DMA((CTX // 2,)),
            pltpu.SemaphoreType.DMA((CTX // 2,)),
        ],
        compiler_params=pltpu.CompilerParams(
            collective_id=0, has_side_effects=True, vmem_limit_bytes=60 * 1024 * 1024
        ),
    )(
        token_ids.reshape(1, ROWS),
        document_ids.reshape(1, ROWS),
        embed_table,
        norm_gain.reshape(1, WIDTH),
        hyena_query,
        hyena_key,
        hyena_filter.T,
        attn_query,
        attn_key,
    )
    return pl.pallas_call(
        turn,
        out_shape=(shape, shape),
        in_specs=[vmem] * 2,
        out_specs=(vmem, vmem),
    )(*(part.reshape(WIDTH, ROWS) for part in sent))


def solution(mesh):
    placed = (
        P("ctx", "ch"),
        P("ctx", "ch"),
        P("ctx"),
        P(None, "ch"),
        P("ch"),
        P("ctx", "ch"),
        P("ctx", "ch"),
        P("ctx", "ch"),
        P("ctx"),
    )
    return jax.shard_map(
        per_device,
        mesh=mesh,
        in_specs=placed,
        out_specs=(P("ctx", "ch"), P("ctx", "ch")),
        check_vma=False,
    )
```

```python
import functools
import math

import jax
import jax.numpy as jnp
from jax import lax
from jax.experimental import pallas as pl
from jax.experimental.pallas import tpu as pltpu
from jax.sharding import PartitionSpec as P

MESH = pl.DeviceIdType.MESH
F32 = jnp.float32
BF16 = jnp.bfloat16

CTX = 32
CH = 4
ROWS = 128
WIDTH = 1024
VOCAB = 512
CHANNELS = 4096
OWN = 32
GROUP = 16
HEAD_DIM = 128
REACH = 2048
EPSILON = 1e-06
MASKED = -1e30
SAME = 8192.0
EXPONENT = HEAD_DIM**-0.5 * math.log2(math.e)

META, SOURCE, GATE, QUERY, KEY, KEY_PAIR, VALUE_PAIR, HOME, ATTN, SQUARES = range(10)


def nt_dot(a, b):
    return lax.dot_general(a, b, (((1,), (1,)), ((), ())), preferred_element_type=F32)


def nn_dot(a, b):
    return jnp.dot(a, b, preferred_element_type=F32)


def halves(value):
    high = value.astype(BF16)
    return high, (value - high.astype(F32)).astype(BF16)


def kernel(
    ids_hbm,
    docs_hbm,
    table_hbm,
    gain_hbm,
    gate_hbm,
    key_hbm,
    filter_hbm,
    attn_query_ref,
    attn_key_ref,
    home_in,
    attn_in,
    ids_ref,
    docs_ref,
    table_ref,
    gain_ref,
    gate_ref,
    key_ref,
    filter_ref,
    squares,
    ids_row,
    scales,
    signals,
    meta_out,
    meta_in,
    source_out,
    source_in,
    gate_out,
    gate_in,
    toeplitz,
    sums,
    values_t,
    keys,
    key_docs,
    queries,
    query_docs,
    attn_t,
    send,
    recv,
    local,
    key_recv,
    query_recv,
):
    me = lax.axis_index("ctx")
    my_ch = lax.axis_index("ch")
    core = lax.rem(me, 2)
    mine = lax.div(me, 2)
    pair = me + 1 - 2 * core

    def remote(src, dst, kind, to, arrived=None):
        return pltpu.make_async_remote_copy(
            src_ref=src,
            dst_ref=dst,
            send_sem=send.at[kind],
            recv_sem=recv.at[kind] if arrived is None else arrived,
            device_id=to,
            device_id_type=MESH,
        )

    def wait_in(ref, kind):
        pltpu.make_async_copy(ref, ref, recv.at[kind]).wait()

    def wait_out(ref, kind):
        pltpu.make_async_copy(ref, ref, send.at[kind]).wait()

    loads = [
        pltpu.make_async_copy(src, dst, local.at[at])
        for at, (src, dst) in enumerate(
            (
                (table_hbm, table_ref),
                (filter_hbm, filter_ref),
                (docs_hbm, docs_ref),
                (ids_hbm, ids_ref),
                (key_hbm, key_ref),
                (gain_hbm, gain_ref),
                (gate_hbm, gate_ref),
            )
        )
    ]
    for load in loads:
        load.start()

    my_keys = keys.at[pl.ds(me * ROWS, ROWS)]
    my_queries = queries.at[mine]
    my_head = pl.ds(pl.multiple_of(lax.div(me, 4) * HEAD_DIM, HEAD_DIM), HEAD_DIM)
    pltpu.make_async_copy(attn_key_ref.at[:, my_head], my_keys, key_recv.at[0]).start()
    pltpu.make_async_copy(attn_query_ref.at[:, my_head], my_queries, query_recv.at[0]).start()

    barrier = pltpu.get_barrier_semaphore()

    @pl.loop(1, CTX)
    def _(r):
        pl.semaphore_signal(
            barrier, inc=1, device_id={"ctx": lax.rem(me + r, CTX)}, device_id_type=MESH
        )

    for r in range(1, CH):
        pl.semaphore_signal(
            barrier, inc=1, device_id={"ch": lax.rem(my_ch + r, CH)}, device_id_type=MESH
        )

    for load in loads[:6]:
        load.wait()

    taps = filter_ref[...]
    docs = docs_ref[...].astype(F32)
    ids = ids_ref[...].astype(F32)
    for d in range(CTX):
        meta_out[d] = jnp.concatenate([taps[2 * d : 2 * d + 2], docs, ids], axis=0)
    meta_in[me] = meta_out[me]

    one_hot_t = (lax.broadcasted_iota(jnp.int32, (VOCAB, ROWS), 0) == ids_ref[...]).astype(F32)
    picked = nn_dot(one_hot_t.T.astype(BF16), table_ref[...])
    product = picked * key_ref[...].astype(F32) * gain_ref[...]
    source_out[...] = product.astype(BF16).T.reshape(CTX, OWN, ROWS)
    source_in[me] = source_out[me]

    by_lane = jnp.zeros((VOCAB, 128), F32)
    for tile in range(WIDTH // 128):
        part = table_ref[:, tile * 128 : (tile + 1) * 128].astype(F32)
        by_lane = by_lane + part * part
    high, low = halves(by_lane)
    ones = jnp.ones((8, 128), BF16)
    squares[my_ch] = nt_dot(ones, high) + nt_dot(ones, low)

    loads[6].wait()
    gate_out[...] = gate_ref[...].T.reshape(CTX, OWN, ROWS)
    gate_in[me] = gate_out[me]

    values_t[64:80, :] = jnp.ones((16, CTX * ROWS), BF16)

    pl.semaphore_wait(barrier, CTX - 1 + CH - 1)

    for r in range(1, CH):
        to = lax.rem(my_ch + r, CH)
        remote(squares.at[my_ch], squares.at[my_ch], SQUARES, {"ch": to}).start()

    @pl.loop(1, CTX)
    def _(r):
        to = lax.rem(me + r, CTX)
        remote(source_out.at[to], source_in.at[me], SOURCE, {"ctx": to}).start()

    @pl.loop(1, CTX)
    def _(r):
        to = lax.rem(me + r, CTX)
        remote(meta_out.at[to], meta_in.at[me], META, {"ctx": to}).start()

    @pl.loop(1, CTX)
    def _(r):
        to = lax.rem(me + r, CTX)
        remote(gate_out.at[to], gate_in.at[me], GATE, {"ctx": to}).start()

    @pl.loop(1, CTX // 2)
    def _(r):
        to = lax.rem(me + 2 * r, CTX)
        head = pl.ds(pl.multiple_of(lax.div(to, 4) * HEAD_DIM, HEAD_DIM), HEAD_DIM)
        remote(attn_key_ref.at[:, head], my_keys, KEY, {"ctx": to}, key_recv.at[r]).start()

    @pl.loop(1, CTX // 2)
    def _(r):
        to = lax.rem(me + 2 * r, CTX)
        head = pl.ds(pl.multiple_of(lax.div(to, 4) * HEAD_DIM, HEAD_DIM), HEAD_DIM)
        remote(
            attn_query_ref.at[:, head], my_queries, QUERY, {"ctx": to}, query_recv.at[r]
        ).start()

    wait_in(meta_in.at[pl.ds(0, CTX - 1)], META)
    down = lax.broadcasted_iota(jnp.int32, (ROWS, ROWS), 0)
    right = lax.broadcasted_iota(jnp.int32, (ROWS, ROWS), 1)
    upper = right >= down

    def turned(n, g):
        row = jnp.broadcast_to(meta_in[n, g : g + 1, :], (ROWS, ROWS))
        return pltpu.roll(row, 0, 1, stride=1, stride_axis=0)

    for g in range(2):

        def build(k, carry):
            before, block_before = carry
            first = turned(2 * k, g)
            second = turned(2 * k + 1, g)
            block = jnp.where(upper, first, before).astype(BF16)
            block_next = jnp.where(upper, second, first).astype(BF16)
            toeplitz[g, k, 0:128, 0:128] = block
            toeplitz[g, k, 128:256, 128:256] = block
            toeplitz[g, k, 0:128, 128:256] = block_next
            toeplitz[g, k, 128:256, 0:128] = block_before
            return second, block_next

        lax.fori_loop(
            0, 16, build, (jnp.zeros((ROWS, ROWS), F32), jnp.zeros((ROWS, ROWS), BF16))
        )

    @pl.loop(0, CTX)
    def _(j):
        which = down.astype(F32) == meta_in[j, 2:3, :]
        key_docs[pl.ds(pl.multiple_of(j * ROWS, ROWS), ROWS)] = (
            which.astype(F32).T.astype(BF16)
        )

    @pl.loop(0, 16)
    def _(q):
        rows = pl.ds(pl.multiple_of((2 * q + core) * ROWS, ROWS), ROWS)
        query_docs[q] = (key_docs[rows].astype(F32) * SAME).astype(BF16)

    for j in range(CTX):
        ids_row[:, j * ROWS : (j + 1) * ROWS] = meta_in[j, 3:4, :].astype(jnp.int32)
    wait_in(squares.at[pl.ds(0, CH - 1)], SQUARES)
    total = (squares[0] + squares[1] + squares[2] + squares[3])[0:1]
    low_digit = lax.broadcasted_iota(jnp.int32, (16, VOCAB), 0)
    token = lax.broadcasted_iota(jnp.int32, (16, VOCAB), 1)
    high, low = halves(jnp.where(lax.rem(token, 16) == low_digit, total, 0.0))
    high_digit = lax.broadcasted_iota(jnp.int32, (32, VOCAB), 0)
    token = lax.broadcasted_iota(jnp.int32, (32, VOCAB), 1)
    gather = (lax.div(token, 16) == high_digit).astype(F32).astype(BF16)
    high, low = halves(nt_dot(high, gather) + nt_dot(low, gather))
    digits = lax.div(ids_row[...], 16)
    chosen = lax.broadcasted_iota(jnp.int32, (32, CTX * ROWS), 0) == digits
    chosen = chosen.astype(F32).astype(BF16)
    choices = nn_dot(high, chosen) + nn_dot(low, chosen)
    digits = lax.rem(ids_row[...], 16)
    chosen = lax.broadcasted_iota(jnp.int32, (16, CTX * ROWS), 0) == digits
    square = jnp.sum(jnp.where(chosen, choices, 0.0), axis=0, keepdims=True)
    scales[...] = lax.rsqrt(square * (1.0 / CHANNELS) + EPSILON)

    wait_in(source_in.at[pl.ds(0, CTX - 1)], SOURCE)
    for j in range(CTX):
        scaled = source_in[j].astype(F32) * scales[:, j * ROWS : (j + 1) * ROWS]
        scaled = scaled.astype(BF16)
        lanes = slice(j % 2 * ROWS, (j % 2 + 1) * ROWS)
        for g in range(2):
            signals[g, j // 2 * GROUP : (j // 2 + 1) * GROUP, lanes] = scaled[
                g * GROUP : (g + 1) * GROUP
            ]
    for g in range(2):
        signal = signals[g]
        sums[g] = nn_dot(signal, toeplitz[g, 0])
        for k in range(1, 16):
            sums[g, 16 * k :] += nn_dot(signal[: 256 - 16 * k], toeplitz[g, k])

    wait_in(gate_in.at[pl.ds(0, CTX - 1)], GATE)
    for g in range(2):
        own = slice(g * GROUP, (g + 1) * GROUP)
        rows = pl.ds(pl.multiple_of(OWN * core + GROUP * g, GROUP), GROUP)
        for j in range(16):
            gate = jnp.concatenate([gate_in[2 * j, own, :], gate_in[2 * j + 1, own, :]], axis=1)
            gated = sums[g, 16 * j : 16 * (j + 1)] * gate.astype(F32)
            values_t[rows, 256 * j : 256 * (j + 1)] = gated.astype(BF16)

    my_rows = pl.ds(pl.multiple_of(OWN * core, OWN), OWN)
    my_values = values_t.at[my_rows, pl.ds(0, CTX * ROWS)]
    remote(my_values, my_values, VALUE_PAIR, {"ctx": pair}).start()

    @pl.loop(0, CTX // 2)
    def _(r):
        source = lax.rem(me + CTX - 2 * r, CTX)
        block = keys.at[pl.ds(source * ROWS, ROWS)]
        pltpu.make_async_copy(block, block, key_recv.at[r]).wait()
        remote(block, block, KEY_PAIR, {"ctx": pair}).start()

    @pl.loop(1, CTX)
    def _(r):
        to = lax.rem(me + r, CTX)
        block = values_t.at[my_rows, pl.ds(pl.multiple_of(to * ROWS, ROWS), ROWS)]
        remote(block, home_in.at[me], HOME, {"ctx": to}).start()

    own_home = pltpu.make_async_copy(
        values_t.at[my_rows, pl.ds(pl.multiple_of(me * ROWS, ROWS), ROWS)], home_in.at[me], local.at[0]
    )
    own_home.start()

    wait_in(source_in, VALUE_PAIR)
    wait_in(keys.at[pl.ds(0, 16 * ROWS)], KEY_PAIR)

    def attend(u, start, blocks, clear):
        rows = pl.ds(pl.multiple_of(start, ROWS), blocks * ROWS)
        some_keys = jnp.concatenate([keys[rows], key_docs[rows]], axis=1)
        both = pl.ds(2 * u, 2)
        some_queries = jnp.concatenate([queries[both], query_docs[both]], axis=2)
        scores = nt_dot(some_keys, some_queries.reshape(2 * ROWS, 256))
        shape = ((blocks - clear) * ROWS, 2 * ROWS)
        at_key = lax.broadcasted_iota(jnp.int32, shape, 0) + (start + clear * ROWS)
        at_query = lax.broadcasted_iota(jnp.int32, shape, 1)
        at_query = jnp.where(at_query >= ROWS, at_query + ROWS, at_query) + (4 * u + core) * ROWS
        late = jnp.where(at_key <= at_query, scores[clear * ROWS :], MASKED)
        if clear:
            late = jnp.concatenate([scores[: clear * ROWS], late], axis=0)
        top = jnp.max(late, axis=0, keepdims=True)
        weights = jnp.exp2((late - top) * EXPONENT).astype(BF16)
        numerator = nn_dot(values_t[:, rows], weights)
        result = (numerator[0:64] * (1.0 / numerator[64:65])).astype(BF16)
        attn_t[2 * u] = result[:, :ROWS]
        attn_t[2 * u + 1] = result[:, ROWS:]

    def give(q):
        block = 2 * q + core

        @pl.when(q == mine)
        def _():
            pltpu.make_async_copy(attn_t.at[q], attn_in.at[mine], local.at[1]).start()

        @pl.when(q != mine)
        def _():
            remote(attn_t.at[q], attn_in.at[mine], ATTN, {"ctx": block}).start()

    @pl.loop(0, 8)
    def _(p):
        u = lax.rem(lax.div(mine + 1, 2) + 7 - p, 8)
        for at in range(2):
            block = queries.at[2 * u + at]
            arrived = query_recv.at[lax.rem(mine + 16 - 2 * u - at, 16)]
            pltpu.make_async_copy(block, block, arrived).wait()

        for early in range(4):

            @pl.when(u == early)
            def _():
                attend(u, 0, 4 * early + 4, 4 * early)

        @pl.when(u >= 4)
        def _():
            attend(u, (4 * u + core) * ROWS - REACH, 19, 16)

        give(2 * u)
        give(2 * u + 1)

    wait_in(home_in.at[pl.ds(0, CTX - 1)], HOME)
    wait_in(attn_in.at[pl.ds(0, 15)], ATTN)

    own_home.wait()
    pltpu.make_async_copy(attn_t.at[mine], attn_in.at[mine], local.at[1]).wait()
    wait_out(squares.at[pl.ds(0, CH - 1)], SQUARES)
    wait_out(meta_in.at[pl.ds(0, CTX - 1)], META)
    wait_out(source_out.at[pl.ds(0, CTX - 1)], SOURCE)
    wait_out(gate_out.at[pl.ds(0, CTX - 1)], GATE)
    wait_out(queries.at[pl.ds(0, 15)], QUERY)
    wait_out(keys.at[pl.ds(0, 15 * ROWS)], KEY)
    wait_out(keys.at[pl.ds(0, 16 * ROWS)], KEY_PAIR)
    wait_out(source_in, VALUE_PAIR)
    wait_out(home_in.at[pl.ds(0, CTX - 1)], HOME)
    wait_out(attn_in.at[pl.ds(0, 15)], ATTN)


def turn(home_ref, attn_ref, hyena_out_ref, attn_out_ref):
    hyena_out_ref[...] = home_ref[...].T
    attn_out_ref[...] = attn_ref[...].T


def per_device(
    hyena_query,
    hyena_key,
    token_ids,
    embed_table,
    norm_gain,
    hyena_filter,
    attn_query,
    attn_key,
    document_ids,
):
    vmem = pl.BlockSpec(memory_space=pltpu.VMEM)
    hbm = pl.BlockSpec(memory_space=pltpu.HBM)
    shape = jax.ShapeDtypeStruct((ROWS, WIDTH), BF16)
    sent = pl.pallas_call(
        kernel,
        out_shape=(
            jax.ShapeDtypeStruct((CTX, OWN, ROWS), BF16),
            jax.ShapeDtypeStruct((16, 64, ROWS), BF16),
        ),
        in_specs=[hbm] * 9,
        out_specs=(hbm, hbm),
        scratch_shapes=[
            pltpu.VMEM((1, ROWS), jnp.int32),
            pltpu.VMEM((1, ROWS), jnp.int32),
            pltpu.VMEM((VOCAB, WIDTH), BF16),
            pltpu.VMEM((1, WIDTH), F32),
            pltpu.VMEM((ROWS, WIDTH), BF16),
            pltpu.VMEM((ROWS, WIDTH), BF16),
            pltpu.VMEM((64, ROWS), F32),
            pltpu.VMEM((CH, 8, VOCAB), F32),
            pltpu.VMEM((1, CTX * ROWS), jnp.int32),
            pltpu.VMEM((1, CTX * ROWS), F32),
            pltpu.VMEM((2, 256, 256), BF16),
            pltpu.VMEM((CTX, 4, ROWS), F32),
            pltpu.VMEM((CTX, 4, ROWS), F32),
            pltpu.VMEM((CTX, OWN, ROWS), BF16),
            pltpu.VMEM((CTX, OWN, ROWS), BF16),
            pltpu.VMEM((CTX, OWN, ROWS), BF16),
            pltpu.VMEM((CTX, OWN, ROWS), BF16),
            pltpu.VMEM((2, 16, 256, 256), BF16),
            pltpu.VMEM((2, 256, 256), F32),
            pltpu.VMEM((80, CTX * ROWS), BF16),
            pltpu.VMEM((CTX * ROWS, 128), BF16),
            pltpu.VMEM((CTX * ROWS, 128), BF16),
            pltpu.VMEM((16, ROWS, HEAD_DIM), BF16),
            pltpu.VMEM((16, ROWS, HEAD_DIM), BF16),
            pltpu.VMEM((16, 64, ROWS), BF16),
            pltpu.SemaphoreType.DMA((10,)),
            pltpu.SemaphoreType.DMA((10,)),
            pltpu.SemaphoreType.DMA((7,)),
            pltpu.SemaphoreType.DMA((CTX // 2,)),
            pltpu.SemaphoreType.DMA((CTX // 2,)),
        ],
        compiler_params=pltpu.CompilerParams(
            collective_id=0, has_side_effects=True, vmem_limit_bytes=60 * 1024 * 1024
        ),
    )(
        token_ids.reshape(1, ROWS),
        document_ids.reshape(1, ROWS),
        embed_table,
        norm_gain.reshape(1, WIDTH),
        hyena_query,
        hyena_key,
        hyena_filter.T,
        attn_query,
        attn_key,
    )
    return pl.pallas_call(
        turn,
        out_shape=(shape, shape),
        in_specs=[vmem] * 2,
        out_specs=(vmem, vmem),
    )(*(part.reshape(WIDTH, ROWS) for part in sent))


def solution(mesh):
    placed = (
        P("ctx", "ch"),
        P("ctx", "ch"),
        P("ctx"),
        P(None, "ch"),
        P("ch"),
        P("ctx", "ch"),
        P("ctx", "ch"),
        P("ctx", "ch"),
        P("ctx"),
    )
    return jax.shard_map(
        per_device,
        mesh=mesh,
        in_specs=placed,
        out_specs=(P("ctx", "ch"), P("ctx", "ch")),
        check_vma=False,
    )
```
